32 devices in a mesh: section: 2 (over x), dp: 16 (over z, y, core).
Axes of the slice: x: 2, y: 2, z: 4, core: 2. Of those that a mesh axis runs over, the one named last changes fastest.
Arguments:
- section_input: bfloat16 [2, 64, 128, 512], P('section', 'dp'), may hold values from -6 to 6
- top_grad: bfloat16 [64, 128, 512], P('dp'), may hold values from -6 to 6
- conv_weight: bfloat16 [2, 3, 512, 512], P('section'), may hold values from -0.15625 to 0.15625
- step_table: bfloat16 [2, 50, 512], P('section'), may hold values from -4 to 4
- timesteps: int32 [64], P('dp'), may hold values from 0 to 49
- dilations: int32 [2], P('section'), may hold values from 1 to 32, as said below
Outputs:
- input_grad: bfloat16 [2, 64, 128, 512], P('section', 'dp')
- weight_grad: bfloat16 [2, 3, 512, 512], P('section')
- table_grad: bfloat16 [2, 50, 512], P('section')
The draws below stay inside these ranges and needn't reach their ends.
Inputs may be any that keep to these rules, and one draw needn't show every extreme that they name: `dilations`: each is a power of two; some section has dilation 32 and some other section dilation 1.
All inputs are finite; a program needn't handle non-finite values.
Results may differ from the reference program's by a relative error of at most 0.014.
Values may be sent and summed in bfloat16 or wider, within the bound.
No kernel may reach another device: no remote copies, remote signals or barrier semaphores. Data moves between devices by JAX's collectives and lax.ppermute only.
A program may use at most 64 MiB of HBM per device.

```python
import math
import jax
import jax.numpy as jnp
from jax import lax

C = 512
NSTEPS = 50
SEQ = 128
DMAX = 32
BATCH = 64
N_SECTION = 2


def draw_dilations(key, part):
    first_key, second_key = jax.random.split(key)
    log_top = DMAX.bit_length() - 1
    powers = jax.random.randint(first_key, (N_SECTION,), 0, log_top + 1)
    values = jnp.power(2, powers).astype(jnp.int32)
    top_pos = jax.random.randint(second_key, (), 0, N_SECTION)
    positions = jnp.arange(N_SECTION, dtype=jnp.int32)
    values = jnp.where(positions == top_pos, DMAX, values)
    values = jnp.where(positions == (top_pos + 1) % N_SECTION, 1, values)
    return values.astype(jnp.int32)


def with_ends(values, rng, smallest, largest):
    longest = values.shape.index(max(values.shape))
    spots = []
    for shift in (0, 1):
        where = [jax.random.randint(jax.random.fold_in(rng, axis), (), 0, length) for axis, length in enumerate(values.shape)]
        where[longest] = (where[longest] + shift) % values.shape[longest]
        spots.append(tuple(where))
    return values.at[spots[0]].set(smallest).at[spots[1]].set(largest)


def level_of(key, extent, cuts, least, largest):
    def one(position, parts):
        draws = jax.random.uniform(jax.random.fold_in(jax.random.fold_in(key, 6), position), (parts,), jnp.float32, least / len(cuts), largest / len(cuts))
        return jnp.repeat(jnp.exp(draws), extent[position] // parts).reshape((-1,) + (1,) * (len(extent) - position - 1))

    factor_of = one(*cuts[0])
    for cut in cuts[1:]:
        factor_of = factor_of * one(*cut)
    return factor_of


def gaussian(stream_key, dims, scale, reach, shards=(), held_as=jnp.bfloat16):
    result = jax.random.normal(stream_key, dims, jnp.float32) * scale
    if len(shards) > 0:
        result = level_of(stream_key, dims, shards, -0.22, 0.18) * result
    return jnp.clip(result, min=-reach, max=reach).astype(held_as)


def setup_inputs(seed: int = 0) -> dict:
    splits = jax.random.split(jax.random.key(seed), 7)
    section_input = gaussian(splits[0], (N_SECTION, BATCH, SEQ, C), 1.0, 6.0, ((0, 2), (1, 16)))
    top_grad = gaussian(splits[1], (BATCH, SEQ, C), 1.0, 6.0, ((0, 16),))
    conv_weight = gaussian(splits[2], (N_SECTION, 3, C, C), (3 * C) ** -0.5, 0.15625, ((0, 2),))
    step_table = gaussian(splits[3], (N_SECTION, NSTEPS, C), 0.7, 4.0, ((0, 2),))
    timesteps = with_ends(jax.random.randint(splits[4], (BATCH,), 0, NSTEPS), jax.random.fold_in(splits[4], 1), 0, NSTEPS - 1).astype(jnp.int32)
    dilations = draw_dilations(jax.random.fold_in(splits[6], 71), 0)
    return {"section_input": section_input, "top_grad": top_grad, "conv_weight": conv_weight, "step_table": step_table, "timesteps": timesteps, "dilations": dilations}


def spread_taps(seq_rows, dilation, orientation):
    bins_count = seq_rows.shape[1]
    padded = jnp.pad(seq_rows, ((0, 0), (DMAX, DMAX), (0, 0)))
    pieces = []
    for tap_num in range(3):
        start = (DMAX + orientation * (tap_num - 1) * dilation).astype(jnp.int32)
        pieces.append(lax.dynamic_slice_in_dim(padded, start, bins_count, 1))
    return jnp.concatenate(pieces, axis=2)

def reference(section_input, top_grad, conv_weight, step_table, timesteps, dilations):
    grad_scale = 1.0 / math.sqrt(BATCH * SEQ)
    onehot = timesteps[:, None] == jnp.arange(NSTEPS, dtype=jnp.int32)[None, :]
    onehot_float = onehot.astype(jnp.float32)
    grad_now = top_grad
    input_list, weight_list, table_list = ([], [], [])
    for section_num in range(N_SECTION - 1, -1, -1):
        conv_kernel = conv_weight[section_num]
        dilation = dilations[section_num]
        step_embed = jnp.dot(onehot.astype(jnp.bfloat16), step_table[section_num], preferred_element_type=jnp.float32)
        mixed_rows = (section_input[section_num].astype(jnp.float32) + step_embed[:, None, :]).astype(jnp.bfloat16)
        fwd_taps = spread_taps(mixed_rows, dilation, 1).reshape(BATCH * SEQ, 3 * C)
        preact = jnp.dot(fwd_taps, conv_kernel.reshape(3 * C, C), preferred_element_type=jnp.float32)
        gate_value = jax.nn.sigmoid(preact)
        upstream = grad_now.reshape(BATCH * SEQ, C).astype(jnp.float32)
        grad_pre = (upstream * gate_value * (1.0 + preact * (1.0 - gate_value))).astype(jnp.bfloat16)
        back_taps = spread_taps(grad_pre.reshape(BATCH, SEQ, C), dilation, -1).reshape(BATCH * SEQ, 3 * C)
        kernel_back = jnp.transpose(conv_kernel, (0, 2, 1)).reshape(3 * C, C)
        grad_mixed = jnp.dot(back_taps, kernel_back, preferred_element_type=jnp.float32)
        grad_now = (upstream + grad_mixed).astype(jnp.bfloat16).reshape(BATCH, SEQ, C)
        weight_total = lax.dot_general(fwd_taps, grad_pre, (((0,), (0,)), ((), ())), preferred_element_type=jnp.float32)
        group_sums = lax.optimization_barrier(jnp.sum(grad_mixed.reshape(BATCH, SEQ, C), axis=1))
        table_total = jnp.dot(onehot_float.T, group_sums, precision=lax.Precision.HIGHEST)
        input_list.append(grad_now)
        weight_list.append((weight_total * grad_scale).astype(jnp.bfloat16).reshape(3, C, C))
        table_list.append((table_total * grad_scale).astype(jnp.bfloat16))
    return (jnp.stack(input_list[::-1]), jnp.stack(weight_list[::-1]), jnp.stack(table_list[::-1]))
```

```python
import functools
import math

import jax
import jax.numpy as jnp
from jax import lax
from jax.experimental import pallas as pl
from jax.experimental.pallas import tpu as pltpu
from jax.sharding import PartitionSpec as P

CHUNKS = 2
F32 = jnp.float32
BF16 = jnp.bfloat16
VMEM = pl.BlockSpec(memory_space=pltpu.VMEM)
SMEM = pl.BlockSpec(memory_space=pltpu.SMEM)
NT = (((1,), (1,)), ((), ()))


def call(kernel, out_shape, args, smem=0, scratch=(), flops=0, aliases=None):
    specs = [SMEM] * smem + [VMEM] * (len(args) - smem)
    moved = sum(a.size * a.dtype.itemsize for a in args)
    moved += sum(math.prod(o.shape) * o.dtype.itemsize for o in out_shape)
    return pl.pallas_call(
        kernel,
        out_shape=out_shape,
        in_specs=specs,
        out_specs=[VMEM] * len(out_shape),
        scratch_shapes=list(scratch),
        input_output_aliases=aliases or {},
        compiler_params=pltpu.CompilerParams(vmem_limit_bytes=48 * 2**20),
        cost_estimate=pl.CostEstimate(flops=flops, bytes_accessed=moved, transcendentals=0),
    )(*args)


def like(shape, dtype):
    return jax.ShapeDtypeStruct(shape, dtype)


def put_taps(values, taps, bins, dilation, orientation):
    rows, cols = values.shape
    place = lax.broadcasted_iota(jnp.int32, (bins, cols), 0)
    taps[:, cols : 2 * cols] = values
    for b in range(rows // bins):
        at = slice(b * bins, (b + 1) * bins)
        group = values[at].astype(F32)
        later = pltpu.roll(group, bins - dilation, 0)
        later = jnp.where(place < bins - dilation, later, 0.0).astype(BF16)
        earlier = pltpu.roll(group, dilation, 0)
        earlier = jnp.where(place >= dilation, earlier, 0.0).astype(BF16)
        first, third = (earlier, later) if orientation == 1 else (later, earlier)
        taps[at, 0:cols] = first
        taps[at, 2 * cols : 3 * cols] = third


def back_product(taps, weight, cols):
    total = None
    for k in range(3):
        part = lax.dot_general(
            taps[:, k * cols : (k + 1) * cols], weight[k], NT, preferred_element_type=F32
        )
        total = part if total is None else total + part
    return total


def first_kernel(ts, dil, x, table, weight, top, slope, h_t, *rest):
    g_out, (taps, tab) = rest[:-2], rest[-2:]
    groups, bins, chans = x.shape
    dilation = dil[0]
    tab[...] = table[...].astype(F32)
    mixed = [
        (x[b].astype(F32) + tab[pl.ds(ts[b], 1), :]).astype(BF16) for b in range(groups)
    ]
    mixed = jnp.concatenate(mixed, axis=0)
    put_taps(mixed, taps, bins, dilation, 1)
    flat = weight[...].reshape(3 * chans, chans)
    y = jnp.dot(taps[...], flat, preferred_element_type=F32)
    gate = jax.nn.sigmoid(y)
    slope[...] = gate * (1.0 + y * (1.0 - gate))
    g = top[...].reshape(groups * bins, chans).astype(F32)
    delta = (g * slope[...]).astype(BF16)
    put_taps(delta, taps, bins, dilation, -1)
    out = (g + back_product(taps, weight, chans)).astype(BF16)
    width = chans // len(g_out)
    for j, ref in enumerate(g_out):
        ref[...] = out[:, j * width : (j + 1) * width]
    h_t[...] = mixed.T


def layer_kernel(bins, dil, slope, weight, g_in, *rest):
    g_out, taps = rest[:-1], rest[-1]
    chans = slope.shape[1]
    g = g_in[...].astype(F32)
    delta = (g * slope[...]).astype(BF16)
    put_taps(delta, taps, bins, dil[0], -1)
    out = (g + back_product(taps, weight, chans)).astype(BF16)
    width = chans // len(g_out)
    for j, ref in enumerate(g_out):
        ref[...] = out[:, j * width : (j + 1) * width]


def weight_kernel(col, scale, flags, dil, top, recv, slope, h_t, g_used, taps, send, keep):
    rows, width = recv.shape
    bins = top.shape[1]
    at_top = flags[0] == 1
    bit = flags[1]
    fresh = top[...].reshape(rows, top.shape[-1])[:, col : col + width]
    g = jnp.where(at_top, fresh.astype(F32), recv[...].astype(F32))
    g_used[...] = g.astype(BF16)
    delta = (g * slope[:, col : col + width]).astype(BF16)
    put_taps(delta, taps, bins, dil[0], -1)
    half = h_t.shape[0] // 2
    for ref, part in ((send, 1 - bit), (keep, bit)):
        left = h_t[pl.ds(pl.multiple_of(part * half, half), half), :]
        prod = jnp.dot(left, taps[...], preferred_element_type=F32)
        ref[:, 0 : 3 * width] = (prod * scale).astype(BF16)


def back_kernel(col, taps, weight, acc):
    width = taps.shape[1] // 3
    acc[...] = back_product(taps, weight[:, :, col : col + width], width)


def last_kernel(
    col, scale, flags, dil, ts, top, recv, slope, h_t, weight, *rest
):
    prior = (len(rest) - 4) // 2
    g_prior, acc = rest[:prior], rest[prior : 2 * prior]
    send, keep, grad, taps = rest[2 * prior :]
    rows, width = recv.shape
    groups, bins, chans = grad.shape
    at_top = flags[0] == 1
    bit = flags[1]
    fresh = top[...].reshape(rows, chans)[:, col : col + width]
    g = jnp.where(at_top, fresh.astype(F32), recv[...].astype(F32))
    delta = (g * slope[:, col : col + width]).astype(BF16)
    put_taps(delta, taps, bins, dil[0], -1)
    dh = back_product(taps, weight[:, :, col : col + width], width)
    for ref in acc:
        dh = dh + ref[...]
    whole = jnp.concatenate([ref[...].astype(F32) for ref in g_prior] + [g], axis=1)
    grad[...] = (whole + dh).astype(BF16).reshape(groups, bins, chans)
    steps = lax.broadcasted_iota(jnp.int32, (128, chans), 0)
    table = jnp.zeros((128, chans), F32)
    for b in range(groups):
        total = jnp.sum(dh[b * bins : (b + 1) * bins], axis=0, keepdims=True)
        table = table + jnp.where(steps == ts[b], total * scale, 0.0)
    table_t = table.T.astype(BF16)
    half = h_t.shape[0] // 2
    for ref, part in ((send, 1 - bit), (keep, bit)):
        left = h_t[pl.ds(pl.multiple_of(part * half, half), half), :]
        prod = jnp.dot(left, taps[...], preferred_element_type=F32)
        ref[:, 0 : 3 * width] = (prod * scale).astype(BF16)
    for ref, part in ((send, 1 - bit), (keep, bit)):
        first = table_t[0:half]
        second = table_t[half : 2 * half]
        ref[:, 3 * width :] = jnp.where(part == 0, first, second)


def fold_kernel(flags, pos, keep, recv, send_out, keep_out):
    half = keep.shape[0] // 2
    for ref, part in ((send_out, 1 - flags[pos]), (keep_out, flags[pos])):
        at = pl.ds(pl.multiple_of(part * half, half), half)
        ref[...] = (keep[at, :].astype(F32) + recv[at, :].astype(F32)).astype(BF16)


def swap(value, bit_num):
    count = lax.axis_size("dp")
    return lax.ppermute(value, "dp", [(i, i ^ (1 << bit_num)) for i in range(count)])


def body(section_input, top_grad, conv_weight, step_table, timesteps, dilations):
    my_section = lax.axis_index("section")
    section_count = lax.axis_size("section")
    dp_count = lax.axis_size("dp")
    dp_bits = dp_count.bit_length() - 1
    me = lax.axis_index("dp")
    x = section_input[0]
    weight = conv_weight[0]
    table = step_table[0]
    groups, bins, chans = x.shape
    rows = groups * bins
    width = chans // CHUNKS
    scale = 1.0 / math.sqrt(groups * dp_count * bins)
    is_top = (my_section == section_count - 1).astype(jnp.int32)
    flags = jnp.stack([is_top] + [(me >> n) & 1 for n in range(dp_bits)]).astype(jnp.int32)
    unit = 2 * rows * chans * chans * 3

    slices = [like((rows, width), BF16)] * CHUNKS
    whole = [like((rows, chans), BF16)]
    ticks = section_count - 1
    slope, h_t, *sent = call(
        first_kernel,
        [like((rows, chans), F32), like((chans, rows), BF16)] + (slices if ticks <= 1 else whole),
        (timesteps, dilations, x, table, weight, top_grad),
        smem=2,
        scratch=[
            pltpu.VMEM((rows, 3 * chans), BF16),
            pltpu.VMEM(table.shape, F32),
        ],
        flops=2 * unit,
    )

    def below(value):
        return lax.ppermute(value, "section", [(i, i - 1) for i in range(1, section_count)])

    for tick in range(1, ticks):
        got = jnp.where(is_top == 1, top_grad.reshape(rows, chans), below(sent[0]))
        sent = call(
            functools.partial(layer_kernel, bins),
            slices if tick == ticks - 1 else whole,
            (dilations, slope, weight, got),
            smem=1,
            scratch=[pltpu.VMEM((rows, 3 * chans), BF16)],
            flops=unit,
        )
    got = [below(value) for value in sent]

    halves = []
    g_used = []
    accs = []
    for c in range(CHUNKS):
        if c < CHUNKS - 1:
            used, taps, send, keep = call(
                functools.partial(weight_kernel, c * width, scale),
                [like((rows, width), BF16), like((rows, 3 * width), BF16)]
                + [like((chans // 2, 3 * width), BF16)] * 2,
                (flags, dilations, top_grad, got[c], slope, h_t),
                smem=2,
                flops=unit // CHUNKS,
            )
            acc = call(
                functools.partial(back_kernel, c * width),
                [like((rows, chans), F32)],
                (taps, weight),
                flops=unit // CHUNKS,
            )[0]
            g_used.append(used)
            accs.append(acc)
        else:
            send, keep, grad = call(
                functools.partial(last_kernel, c * width, scale),
                [like((chans // 2, 3 * width + 128), BF16)] * 2 + [like(x.shape, BF16)],
                (flags, dilations, timesteps, top_grad, got[c], slope, h_t, weight)
                + tuple(g_used)
                + tuple(accs),
                smem=3,
                scratch=[pltpu.VMEM((rows, 3 * width), BF16)],
                flops=2 * unit // CHUNKS,
            )
        halves.append((send, keep))

    order = None
    counts = []
    pieces = []
    for send, keep in halves:
        cols = keep.shape[1]
        for n in range(1, dp_bits - 1):
            recv = swap(send, n - 1)
            half = [like((keep.shape[0] // 2, cols), BF16)] * 2
            fold = lambda flags_ref, *refs, pos=1 + n: fold_kernel(flags_ref, pos, *refs)
            send, keep = call(fold, half, (flags, keep, recv), smem=1)
        keep = (keep.astype(F32) + swap(send, dp_bits - 2).astype(F32)).astype(BF16)
        own = (keep.astype(F32) + swap(keep, dp_bits - 1).astype(F32)).astype(BF16)
        held = [(own, [0])]
        for n in range(dp_bits - 2, 0, -1):
            message = jnp.concatenate([v for v, _ in held], axis=0) if len(held) > 1 else held[0][0]
            offsets = [o for _, offs in held for o in offs]
            held.append((swap(message, n), [o ^ (1 << n) for o in offsets]))
        held = held + [(swap(v, 0), [o ^ 1 for o in offs]) for v, offs in held]
        pieces += [v for v, _ in held]
        order = [offs for _, offs in held]
        counts.append(len(held))

    weight_out, table_t = call(
        lambda flags_ref, *refs: assemble_kernel(order, counts, dp_bits, flags_ref, *refs),
        [like(weight.shape, BF16), like((chans, 128), BF16)],
        (flags,) + tuple(pieces),
        smem=1,
    )
    table_out = table_t.T[: table.shape[0]]
    return (grad[None], weight_out[None], table_out[None])


def assemble_kernel(order, counts, dp_bits, flags, *refs):
    weight_out, table_out = refs[-2], refs[-1]
    pieces = refs[:-2]
    chans = weight_out.shape[1]
    width = chans // len(counts)
    at = 0
    for c, count in enumerate(counts):
        for n in range(count):
            ref = pieces[at]
            at += 1
            size = ref.shape[0] // len(order[n])
            for slot, offset in enumerate(order[n]):
                block = 0
                for bit_num in range(dp_bits - 1):
                    bit = flags[1 + bit_num]
                    block = block * 2 + (1 - bit if (offset >> bit_num) & 1 else bit)
                row = pl.ds(pl.multiple_of(block * size, size), size)
                here = slice(slot * size, (slot + 1) * size)
                for k in range(3):
                    weight_out[k, row, c * width : (c + 1) * width] = ref[
                        here, k * width : (k + 1) * width
                    ]
                if ref.shape[1] > 3 * width:
                    table_out[row, :] = ref[here, 3 * width :]


def solution(mesh):
    placed = (
        P("section", "dp", None, None),
        P("dp", None, None),
        P("section", None, None, None),
        P("section", None, None),
        P("dp"),
        P("section"),
    )
    return jax.shard_map(
        body,
        mesh=mesh,
        in_specs=placed,
        out_specs=(
            P("section", "dp", None, None),
            P("section", None, None, None),
            P("section", None, None),
        ),
        check_vma=False,
    )
```

```python
import functools
import math

import jax
import jax.numpy as jnp
from jax import lax
from jax.experimental import pallas as pl
from jax.experimental.pallas import tpu as pltpu
from jax.sharding import PartitionSpec as P

CHUNKS = 2
F32 = jnp.float32
BF16 = jnp.bfloat16
VMEM = pl.BlockSpec(memory_space=pltpu.VMEM)
SMEM = pl.BlockSpec(memory_space=pltpu.SMEM)
HBM = pl.BlockSpec(memory_space=pltpu.HBM)
NT = (((1,), (1,)), ((), ()))


def call(kernel, out_shape, args, smem=0, far=0, scratch=(), flops=0):
    specs = [SMEM] * smem + [HBM] * far + [VMEM] * (len(args) - smem - far)
    moved = sum(a.size * a.dtype.itemsize for a in args)
    moved += sum(math.prod(o.shape) * o.dtype.itemsize for o in out_shape)
    return pl.pallas_call(
        kernel,
        out_shape=out_shape,
        in_specs=specs,
        out_specs=[VMEM] * len(out_shape),
        scratch_shapes=list(scratch),
        compiler_params=pltpu.CompilerParams(vmem_limit_bytes=48 * 2**20),
        cost_estimate=pl.CostEstimate(flops=flops, bytes_accessed=moved, transcendentals=0),
    )(*args)


def is_top():
    return lax.axis_index("section") == lax.axis_size("section") - 1


def dp_bit(n):
    return lax.rem(lax.div(lax.axis_index("dp"), 1 << n), 2)


def like(shape, dtype):
    return jax.ShapeDtypeStruct(shape, dtype)


def put_taps(values, taps, bins, dilation, orientation):
    rows, cols = values.shape
    place = lax.broadcasted_iota(jnp.int32, (bins, cols), 0)
    taps[:, cols : 2 * cols] = values
    for b in range(rows // bins):
        at = slice(b * bins, (b + 1) * bins)
        group = values[at].astype(F32)
        later = pltpu.roll(group, bins - dilation, 0)
        later = jnp.where(place < bins - dilation, later, 0.0).astype(BF16)
        earlier = pltpu.roll(group, dilation, 0)
        earlier = jnp.where(place >= dilation, earlier, 0.0).astype(BF16)
        first, third = (earlier, later) if orientation == 1 else (later, earlier)
        taps[at, 0:cols] = first
        taps[at, 2 * cols : 3 * cols] = third


def back_product(taps, weight, cols):
    total = None
    for k in range(3):
        part = lax.dot_general(
            taps[:, k * cols : (k + 1) * cols], weight[k], NT, preferred_element_type=F32
        )
        total = part if total is None else total + part
    return total


def first_kernel(
    dil, ts, x, table, weight, top, slope, mixed, taps, weight_v, top_v, hot, g_out, *scratch
):
    ts_s, x_v, table_v, tab, sems = scratch
    pairs = ((ts, ts_s), (x, x_v), (table, table_v), (weight, weight_v), (top, top_v))
    copies = [pltpu.make_async_copy(a, b, sems.at[n]) for n, (a, b) in enumerate(pairs)]
    for copy in copies:
        copy.start()
    groups, bins, chans = x.shape
    for copy in copies[:3]:
        copy.wait()
    tab[...] = table_v[...].astype(F32)
    for b in range(groups):
        row = x_v[b].astype(F32) + tab[pl.ds(ts_s[b], 1), :]
        mixed[b * bins : (b + 1) * bins, :] = row.astype(BF16)
    put_taps(mixed[...], taps, bins, dil[0], 1)
    steps = lax.broadcasted_iota(jnp.int32, hot.shape, 0)
    lanes = lax.broadcasted_iota(jnp.int32, hot.shape, 1)
    marks = jnp.zeros(hot.shape, F32)
    for b in range(groups):
        marks = jnp.where((lanes == b) & (steps == ts_s[b]), 1.0, marks)
    hot[...] = marks
    copies[3].wait()
    flat = weight_v[...].reshape(3 * chans, chans)
    y = jnp.dot(taps[...], flat, preferred_element_type=F32)
    gate = jax.nn.sigmoid(y)
    slope[...] = gate * (1.0 + y * (1.0 - gate))
    copies[4].wait()
    g = top_v[...].reshape(groups * bins, chans).astype(F32)
    delta = (g * slope[...]).astype(BF16)
    put_taps(delta, taps, bins, dil[0], -1)
    width = g_out.shape[1]
    dh = back_product(taps, weight_v[:, 0:width, :], chans)
    g_out[...] = (g[:, 0:width] + dh).astype(BF16)


def second_kernel(start, mixed, taps, weight, top, g_out, h_t):
    width = g_out.shape[1]
    chans = mixed.shape[1]
    dh = back_product(taps, weight[:, start : start + width, :], chans)
    g = top[...].reshape(mixed.shape)[:, start : start + width]
    g_out[...] = (g.astype(F32) + dh).astype(BF16)
    h_t[...] = mixed[...].T


def layer_kernel(bins, dil, slope, weight, top, *rest):
    g_in, g_out, taps = rest[:CHUNKS], rest[CHUNKS:-1], rest[-1]
    chans = slope.shape[1]
    got = jnp.concatenate([ref[...] for ref in g_in], axis=1)
    fresh = top[...].reshape(got.shape)
    g = jnp.where(is_top(), fresh.astype(F32), got.astype(F32))
    delta = (g * slope[...]).astype(BF16)
    put_taps(delta, taps, bins, dil[0], -1)
    out = (g + back_product(taps, weight, chans)).astype(BF16)
    at = 0
    for ref in g_out:
        ref[...] = out[:, at : at + ref.shape[1]]
        at += ref.shape[1]


def weight_halves(h_t, taps, scale, send, keep, cols):
    half = h_t.shape[0] // 2
    bit = dp_bit(0)
    for ref, part in ((send, 1 - bit), (keep, bit)):
        left = h_t[pl.ds(pl.multiple_of(part * half, half), half), :]
        prod = jnp.dot(left, taps[...], preferred_element_type=F32)
        ref[:, 0:cols] = (prod * scale).astype(BF16)


def weight_kernel(col, scale, dil, top, recv, slope, h_t, g_used, taps, send, keep):
    rows, width = recv.shape
    fresh = top[...].reshape(rows, top.shape[-1])[:, col : col + width]
    g = jnp.where(is_top(), fresh.astype(F32), recv[...].astype(F32))
    g_used[...] = g.astype(BF16)
    delta = (g * slope[:, col : col + width]).astype(BF16)
    put_taps(delta, taps, top.shape[1], dil[0], -1)
    weight_halves(h_t, taps, scale, send, keep, 3 * width)


def back_kernel(col, taps, weight, acc):
    width = taps.shape[1] // 3
    acc[...] = back_product(taps, weight[:, :, col : col + width], width)


def last_kernel(col, scale, dil, top, recv, slope, h_t, weight, hot, *rest):
    prior = (len(rest) - 4) // 2
    g_prior, acc = rest[:prior], rest[prior : 2 * prior]
    send, keep, grad, taps = rest[2 * prior :]
    rows, width = recv.shape
    groups, bins, chans = grad.shape
    fresh = top[...].reshape(rows, chans)[:, col : col + width]
    g = jnp.where(is_top(), fresh.astype(F32), recv[...].astype(F32))
    delta = (g * slope[:, col : col + width]).astype(BF16)
    put_taps(delta, taps, bins, dil[0], -1)
    dh = back_product(taps, weight[:, :, col : col + width], width)
    for ref in acc:
        dh = dh + ref[...]
    whole = jnp.concatenate([ref[...].astype(F32) for ref in g_prior] + [g], axis=1)
    grad[...] = (whole + dh).astype(BF16).reshape(groups, bins, chans)
    table = jnp.zeros((hot.shape[0], chans), F32)
    for b in range(groups):
        total = jnp.sum(dh[b * bins : (b + 1) * bins], axis=0, keepdims=True)
        table = table + hot[:, b : b + 1] * (total * scale)
    table_t = table.T.astype(BF16)
    weight_halves(h_t, taps, scale, send, keep, 3 * width)
    half = chans // 2
    bit = dp_bit(0)
    for ref, part in ((send, 1 - bit), (keep, bit)):
        ref[:, 3 * width :] = jnp.where(part == 0, table_t[0:half], table_t[half:])


def fold_kernel(bit_num, keep, recv, send_out, keep_out):
    half = keep.shape[0] // 2
    bit = dp_bit(bit_num)
    for ref, part in ((send_out, 1 - bit), (keep_out, bit)):
        at = pl.ds(pl.multiple_of(part * half, half), half)
        ref[...] = (keep[at, :].astype(F32) + recv[at, :].astype(F32)).astype(BF16)


def assemble_kernel(plans, *refs):
    weight_out, table_out, table_t = refs[-3:]
    pieces = list(refs[:-3])
    col = 0
    for halvings, lists in plans:
        for offsets in lists:
            ref = pieces.pop(0)
            size = ref.shape[0] // len(offsets)
            for slot, offset in enumerate(offsets):
                block = 0
                for n in halvings:
                    bit = dp_bit(n)
                    block = block * 2 + (1 - bit if (offset >> n) & 1 else bit)
                row = pl.ds(pl.multiple_of(block * size, size), size)
                here = slice(slot * size, (slot + 1) * size)
                width = ref.shape[1] // 3 // 128 * 128
                for k in range(3):
                    weight_out[k, row, col : col + width] = ref[here, k * width : (k + 1) * width]
                if ref.shape[1] > 3 * width:
                    table_t[row, :] = ref[here, 3 * width :].astype(F32)
        col += width
    table_out[...] = table_t[...].T[: table_out.shape[0]].astype(BF16)


def swap(value, bit_num):
    count = lax.axis_size("dp")
    return lax.ppermute(value, "dp", [(i, i ^ (1 << bit_num)) for i in range(count)])


def body(section_input, top_grad, conv_weight, step_table, timesteps, dilations):
    section_count = lax.axis_size("section")
    dp_count = lax.axis_size("dp")
    dp_bits = dp_count.bit_length() - 1
    x = section_input[0]
    weight = conv_weight[0]
    table = step_table[0]
    groups, bins, chans = x.shape
    rows = groups * bins
    width = chans // CHUNKS
    scale = 1.0 / math.sqrt(groups * dp_count * bins)
    unit = 2 * rows * chans * chans * 3

    slope, mixed, taps, weight, top, hot, first = call(
        first_kernel,
        [
            like((rows, chans), F32),
            like((rows, chans), BF16),
            like((rows, 3 * chans), BF16),
            like(weight.shape, BF16),
            like(x.shape, BF16),
            like((128, 128), F32),
            like((rows, width), BF16),
        ],
        (dilations, timesteps, x, table, weight, top_grad),
        smem=1,
        far=5,
        scratch=[
            pltpu.SMEM(timesteps.shape, jnp.int32),
            pltpu.VMEM(x.shape, BF16),
            pltpu.VMEM(table.shape, BF16),
            pltpu.VMEM(table.shape, F32),
            pltpu.SemaphoreType.DMA((5,)),
        ],
        flops=3 * unit // 2,
    )

    def below(value):
        return lax.ppermute(value, "section", [(i, i - 1) for i in range(1, section_count)])

    second, h_t = call(
        functools.partial(second_kernel, width),
        [like((rows, chans - width), BF16), like((chans, rows), BF16)],
        (mixed, taps, weight, top),
        flops=unit // 2,
    )
    got = [below(first), below(second)]
    for _ in range(section_count - 2):
        sent = call(
            functools.partial(layer_kernel, bins),
            [like(v.shape, BF16) for v in got],
            (dilations, slope, weight, top) + tuple(got),
            smem=1,
            scratch=[pltpu.VMEM((rows, 3 * chans), BF16)],
            flops=unit,
        )
        got = [below(value) for value in sent]

    used, taps, send, keep = call(
        functools.partial(weight_kernel, 0, scale),
        [like((rows, width), BF16), like((rows, 3 * width), BF16)]
        + [like((chans // 2, 3 * width), BF16)] * 2,
        (dilations, top, got[0], slope, h_t),
        smem=1,
        flops=unit // 2,
    )
    acc = call(
        functools.partial(back_kernel, 0),
        [like((rows, chans), F32)],
        (taps, weight),
        flops=unit // 2,
    )[0]
    send_2, keep_2, grad = call(
        functools.partial(last_kernel, width, scale),
        [like((chans // 2, 3 * width + 128), BF16)] * 2 + [like(x.shape, BF16)],
        (dilations, top, got[1], slope, h_t, weight, hot, used, acc),
        smem=1,
        scratch=[pltpu.VMEM((rows, 3 * width), BF16)],
        flops=unit,
    )

    inner = list(range(1, dp_bits - 1))
    plans = []
    pieces = []
    for send, keep, order in ((send, keep, inner), (send_2, keep_2, inner[::-1])):
        cols = keep.shape[1]
        at = 0
        for n in order:
            half = [like((keep.shape[0] // 2, cols), BF16)] * 2
            send, keep = call(functools.partial(fold_kernel, n), half, (keep, swap(send, at)))
            at = n
        keep = (keep.astype(F32) + swap(send, at).astype(F32)).astype(BF16)
        own = (keep.astype(F32) + swap(keep, dp_bits - 1).astype(F32)).astype(BF16)
        held = [(own, [0])]
        for n in order[::-1]:
            message = jnp.concatenate([v for v, _ in held], axis=0) if len(held) > 1 else own
            offsets = [o for _, offs in held for o in offs]
            held.append((swap(message, n), [o ^ (1 << n) for o in offsets]))
        held = held + [(swap(v, 0), [o ^ 1 for o in offs]) for v, offs in held]
        pieces += [v for v, _ in held]
        plans.append(([0] + order, [offs for _, offs in held]))

    weight_out, table_out = call(
        functools.partial(assemble_kernel, plans),
        [like(weight.shape, BF16), like(table.shape, BF16)],
        tuple(pieces),
        scratch=[pltpu.VMEM((chans, 128), F32)],
    )
    return (grad[None], weight_out[None], table_out[None])


def solution(mesh):
    placed = (
        P("section", "dp", None, None),
        P("dp", None, None),
        P("section", None, None, None),
        P("section", None, None),
        P("dp"),
        P("section"),
    )
    return jax.shard_map(
        body,
        mesh=mesh,
        in_specs=placed,
        out_specs=(
            P("section", "dp", None, None),
            P("section", None, None, None),
            P("section", None, None),
        ),
        check_vma=False,
    )
```

```python
import functools
import math

import jax
import jax.numpy as jnp
from jax import lax
from jax.experimental import pallas as pl
from jax.experimental.pallas import tpu as pltpu
from jax.sharding import PartitionSpec as P

CHUNKS = 2
F32 = jnp.float32
BF16 = jnp.bfloat16
VMEM = pl.BlockSpec(memory_space=pltpu.VMEM)
SMEM = pl.BlockSpec(memory_space=pltpu.SMEM)
HBM = pl.BlockSpec(memory_space=pltpu.HBM)
NT = (((1,), (1,)), ((), ()))


def call(kernel, out_shape, args, smem=0, far=0, scratch=(), flops=0):
    specs = [SMEM] * smem + [HBM] * far + [VMEM] * (len(args) - smem - far)
    moved = sum(a.size * a.dtype.itemsize for a in args)
    moved += sum(math.prod(o.shape) * o.dtype.itemsize for o in out_shape)
    return pl.pallas_call(
        kernel,
        out_shape=out_shape,
        in_specs=specs,
        out_specs=[VMEM] * len(out_shape),
        scratch_shapes=list(scratch),
        compiler_params=pltpu.CompilerParams(vmem_limit_bytes=48 * 2**20),
        cost_estimate=pl.CostEstimate(flops=flops, bytes_accessed=moved, transcendentals=0),
    )(*args)


def is_top():
    return lax.axis_index("section") == lax.axis_size("section") - 1


def dp_bit(n):
    return lax.rem(lax.div(lax.axis_index("dp"), 1 << n), 2)


def like(shape, dtype):
    return jax.ShapeDtypeStruct(shape, dtype)


def put_taps(values, taps, bins, dilation, orientation):
    rows, cols = values.shape
    place = lax.broadcasted_iota(jnp.int32, (bins, cols), 0)
    taps[:, cols : 2 * cols] = values
    for b in range(rows // bins):
        at = slice(b * bins, (b + 1) * bins)
        group = values[at].astype(F32)
        later = pltpu.roll(group, bins - dilation, 0)
        later = jnp.where(place < bins - dilation, later, 0.0).astype(BF16)
        earlier = pltpu.roll(group, dilation, 0)
        earlier = jnp.where(place >= dilation, earlier, 0.0).astype(BF16)
        first, third = (earlier, later) if orientation == 1 else (later, earlier)
        taps[at, 0:cols] = first
        taps[at, 2 * cols : 3 * cols] = third


def back_product(taps, weight, cols):
    total = None
    for k in range(3):
        part = lax.dot_general(
            taps[:, k * cols : (k + 1) * cols], weight[k], NT, preferred_element_type=F32
        )
        total = part if total is None else total + part
    return total


def first_kernel(
    dil, ts, x, table, weight, top, slope, mixed, taps, weight_v, top_v, hot, g_out, *scratch
):
    ts_s, x_v, table_v, tab, sems = scratch
    pairs = ((ts, ts_s), (x, x_v), (table, table_v), (weight, weight_v), (top, top_v))
    copies = [pltpu.make_async_copy(a, b, sems.at[n]) for n, (a, b) in enumerate(pairs)]
    for copy in copies:
        copy.start()
    groups, bins, chans = x.shape
    for copy in copies[:3]:
        copy.wait()
    tab[...] = table_v[...].astype(F32)
    for b in range(groups):
        row = x_v[b].astype(F32) + tab[pl.ds(ts_s[b], 1), :]
        mixed[b * bins : (b + 1) * bins, :] = row.astype(BF16)
    put_taps(mixed[...], taps, bins, dil[0], 1)
    steps = lax.broadcasted_iota(jnp.int32, hot.shape, 0)
    lanes = lax.broadcasted_iota(jnp.int32, hot.shape, 1)
    marks = jnp.zeros(hot.shape, F32)
    for b in range(groups):
        marks = jnp.where((lanes == b) & (steps == ts_s[b]), 1.0, marks)
    hot[...] = marks
    copies[3].wait()
    flat = weight_v[...].reshape(3 * chans, chans)
    y = jnp.dot(taps[...], flat, preferred_element_type=F32)
    gate = jax.nn.sigmoid(y)
    slope[...] = gate * (1.0 + y * (1.0 - gate))
    copies[4].wait()
    g = top_v[...].reshape(groups * bins, chans).astype(F32)
    delta = (g * slope[...]).astype(BF16)
    put_taps(delta, taps, bins, dil[0], -1)
    width = g_out.shape[1]
    dh = back_product(taps, weight_v[:, 0:width, :], chans)
    g_out[...] = (g[:, 0:width] + dh).astype(BF16)


def second_kernel(start, mixed, taps, weight, top, g_out, h_t):
    width = g_out.shape[1]
    chans = mixed.shape[1]
    dh = back_product(taps, weight[:, start : start + width, :], chans)
    g = top[...].reshape(mixed.shape)[:, start : start + width]
    g_out[...] = (g.astype(F32) + dh).astype(BF16)
    h_t[...] = mixed[...].T


def layer_kernel(bins, dil, slope, weight, top, *rest):
    g_in, g_out, taps = rest[:CHUNKS], rest[CHUNKS:-1], rest[-1]
    chans = slope.shape[1]
    got = jnp.concatenate([ref[...] for ref in g_in], axis=1)
    fresh = top[...].reshape(got.shape)
    g = jnp.where(is_top(), fresh.astype(F32), got.astype(F32))
    delta = (g * slope[...]).astype(BF16)
    put_taps(delta, taps, bins, dil[0], -1)
    out = (g + back_product(taps, weight, chans)).astype(BF16)
    at = 0
    for ref in g_out:
        ref[...] = out[:, at : at + ref.shape[1]]
        at += ref.shape[1]


def weight_halves(h_t, taps, scale, send, keep, cols):
    half = h_t.shape[0] // 2
    bit = dp_bit(0)
    for ref, part in ((send, 1 - bit), (keep, bit)):
        left = h_t[pl.ds(pl.multiple_of(part * half, half), half), :]
        prod = jnp.dot(left, taps[...], preferred_element_type=F32)
        ref[:, 0:cols] = (prod * scale).astype(BF16)


def weight_kernel(col, scale, dil, top, recv, slope, h_t, g_used, taps, send, keep):
    rows, width = recv.shape
    fresh = top[...].reshape(rows, top.shape[-1])[:, col : col + width]
    g = jnp.where(is_top(), fresh.astype(F32), recv[...].astype(F32))
    g_used[...] = g.astype(BF16)
    delta = (g * slope[:, col : col + width]).astype(BF16)
    put_taps(delta, taps, top.shape[1], dil[0], -1)
    weight_halves(h_t, taps, scale, send, keep, 3 * width)


def back_kernel(col, taps, weight, acc):
    width = taps.shape[1] // 3
    acc[...] = back_product(taps, weight[:, :, col : col + width], width)


def last_kernel(col, scale, dil, top, recv, slope, h_t, weight, hot, *rest):
    prior = (len(rest) - 4) // 2
    g_prior, acc = rest[:prior], rest[prior : 2 * prior]
    send, keep, grad, taps = rest[2 * prior :]
    rows, width = recv.shape
    groups, bins, chans = grad.shape
    fresh = top[...].reshape(rows, chans)[:, col : col + width]
    g = jnp.where(is_top(), fresh.astype(F32), recv[...].astype(F32))
    delta = (g * slope[:, col : col + width]).astype(BF16)
    put_taps(delta, taps, bins, dil[0], -1)
    dh = back_product(taps, weight[:, :, col : col + width], width)
    for ref in acc:
        dh = dh + ref[...]
    whole = jnp.concatenate([ref[...].astype(F32) for ref in g_prior] + [g], axis=1)
    grad[...] = (whole + dh).astype(BF16).reshape(groups, bins, chans)
    table = jnp.zeros((hot.shape[0], chans), F32)
    for b in range(groups):
        total = jnp.sum(dh[b * bins : (b + 1) * bins], axis=0, keepdims=True)
        table = table + hot[:, b : b + 1] * (total * scale)
    table_t = table.T.astype(BF16)
    weight_halves(h_t, taps, scale, send, keep, 3 * width)
    half = chans // 2
    bit = dp_bit(0)
    for ref, part in ((send, 1 - bit), (keep, bit)):
        ref[:, 3 * width :] = jnp.where(part == 0, table_t[0:half], table_t[half:])


def fold_kernel(bit_num, keep, recv, send_out, keep_out):
    half = keep.shape[0] // 2
    bit = dp_bit(bit_num)
    for ref, part in ((send_out, 1 - bit), (keep_out, bit)):
        at = pl.ds(pl.multiple_of(part * half, half), half)
        ref[...] = (keep[at, :].astype(F32) + recv[at, :].astype(F32)).astype(BF16)


def assemble_kernel(plans, *refs):
    weight_out, table_out, table_t = refs[-3:]
    pieces = list(refs[:-3])
    col = 0
    for halvings, lists in plans:
        for offsets in lists:
            ref = pieces.pop(0)
            size = ref.shape[0] // len(offsets)
            for slot, offset in enumerate(offsets):
                block = 0
                for n in halvings:
                    bit = dp_bit(n)
                    block = block * 2 + (1 - bit if (offset >> n) & 1 else bit)
                row = pl.ds(pl.multiple_of(block * size, size), size)
                here = slice(slot * size, (slot + 1) * size)
                width = ref.shape[1] // 3 // 128 * 128
                for k in range(3):
                    weight_out[k, row, col : col + width] = ref[here, k * width : (k + 1) * width]
                if ref.shape[1] > 3 * width:
                    table_t[row, :] = ref[here, 3 * width :].astype(F32)
        col += width
    table_out[...] = table_t[...].T[: table_out.shape[0]].astype(BF16)


def swap(value, bit_num):
    count = lax.axis_size("dp")
    return lax.ppermute(value, "dp", [(i, i ^ (1 << bit_num)) for i in range(count)])


def body(section_input, top_grad, conv_weight, step_table, timesteps, dilations):
    section_count = lax.axis_size("section")
    dp_count = lax.axis_size("dp")
    dp_bits = dp_count.bit_length() - 1
    x = section_input[0]
    weight = conv_weight[0]
    table = step_table[0]
    groups, bins, chans = x.shape
    rows = groups * bins
    width = chans // CHUNKS
    scale = 1.0 / math.sqrt(groups * dp_count * bins)
    unit = 2 * rows * chans * chans * 3

    slope, mixed, taps, weight, top, hot, first = call(
        first_kernel,
        [
            like((rows, chans), F32),
            like((rows, chans), BF16),
            like((rows, 3 * chans), BF16),
            like(weight.shape, BF16),
            like(x.shape, BF16),
            like((128, 128), F32),
            like((rows, width), BF16),
        ],
        (dilations,) + tuple(pltpu.with_memory_space_constraint(v, pltpu.HBM) for v in (timesteps, x, table, weight, top_grad)),
        smem=1,
        far=5,
        scratch=[
            pltpu.SMEM(timesteps.shape, jnp.int32),
            pltpu.VMEM(x.shape, BF16),
            pltpu.VMEM(table.shape, BF16),
            pltpu.VMEM(table.shape, F32),
            pltpu.SemaphoreType.DMA((5,)),
        ],
        flops=3 * unit // 2,
    )

    def below(value):
        return lax.ppermute(value, "section", [(i, i - 1) for i in range(1, section_count)])

    second, h_t = call(
        functools.partial(second_kernel, width),
        [like((rows, chans - width), BF16), like((chans, rows), BF16)],
        (mixed, taps, weight, top),
        flops=unit // 2,
    )
    got = [below(first), below(second)]
    for _ in range(section_count - 2):
        sent = call(
            functools.partial(layer_kernel, bins),
            [like(v.shape, BF16) for v in got],
            (dilations, slope, weight, top) + tuple(got),
            smem=1,
            scratch=[pltpu.VMEM((rows, 3 * chans), BF16)],
            flops=unit,
        )
        got = [below(value) for value in sent]

    used, taps, send, keep = call(
        functools.partial(weight_kernel, 0, scale),
        [like((rows, width), BF16), like((rows, 3 * width), BF16)]
        + [like((chans // 2, 3 * width), BF16)] * 2,
        (dilations, top, got[0], slope, h_t),
        smem=1,
        flops=unit // 2,
    )
    acc = call(
        functools.partial(back_kernel, 0),
        [like((rows, chans), F32)],
        (taps, weight),
        flops=unit // 2,
    )[0]
    send_2, keep_2, grad = call(
        functools.partial(last_kernel, width, scale),
        [like((chans // 2, 3 * width + 128), BF16)] * 2 + [like(x.shape, BF16)],
        (dilations, top, got[1], slope, h_t, weight, hot, used, acc),
        smem=1,
        scratch=[pltpu.VMEM((rows, 3 * width), BF16)],
        flops=unit,
    )

    inner = list(range(1, dp_bits - 1))
    plans = []
    pieces = []
    for send, keep, order in ((send, keep, inner), (send_2, keep_2, inner[::-1])):
        cols = keep.shape[1]
        at = 0
        for n in order:
            half = [like((keep.shape[0] // 2, cols), BF16)] * 2
            send, keep = call(functools.partial(fold_kernel, n), half, (keep, swap(send, at)))
            at = n
        keep = (keep.astype(F32) + swap(send, at).astype(F32)).astype(BF16)
        own = (keep.astype(F32) + swap(keep, dp_bits - 1).astype(F32)).astype(BF16)
        held = [(own, [0])]
        for n in order[::-1]:
            message = jnp.concatenate([v for v, _ in held], axis=0) if len(held) > 1 else own
            offsets = [o for _, offs in held for o in offs]
            held.append((swap(message, n), [o ^ (1 << n) for o in offsets]))
        held = held + [(swap(v, 0), [o ^ 1 for o in offs]) for v, offs in held]
        pieces += [v for v, _ in held]
        plans.append(([0] + order, [offs for _, offs in held]))

    weight_out, table_out = call(
        functools.partial(assemble_kernel, plans),
        [like(weight.shape, BF16), like(table.shape, BF16)],
        tuple(pieces),
        scratch=[pltpu.VMEM((chans, 128), F32)],
    )
    return (grad[None], weight_out[None], table_out[None])


def solution(mesh):
    placed = (
        P("section", "dp", None, None),
        P("dp", None, None),
        P("section", None, None, None),
        P("section", None, None),
        P("dp"),
        P("section"),
    )
    return jax.shard_map(
        body,
        mesh=mesh,
        in_specs=placed,
        out_specs=(
            P("section", "dp", None, None),
            P("section", None, None, None),
            P("section", None, None),
        ),
        check_vma=False,
    )
```

```python
import functools
import math

import jax
import jax.numpy as jnp
from jax import lax
from jax.experimental import pallas as pl
from jax.experimental.pallas import tpu as pltpu
from jax.sharding import PartitionSpec as P

SENT = (256, 256)
PARTS = 2
F32 = jnp.float32
BF16 = jnp.bfloat16
VMEM = pl.BlockSpec(memory_space=pltpu.VMEM)
SMEM = pl.BlockSpec(memory_space=pltpu.SMEM)
HBM = pl.BlockSpec(memory_space=pltpu.HBM)
NT = (((1,), (1,)), ((), ()))


def call(kernel, out_shape, args, smem=0, far=0, scratch=(), flops=0):
    specs = [SMEM] * smem + [HBM] * far + [VMEM] * (len(args) - smem - far)
    moved = sum(a.size * a.dtype.itemsize for a in args)
    moved += sum(math.prod(o.shape) * o.dtype.itemsize for o in out_shape)
    return pl.pallas_call(
        kernel,
        out_shape=out_shape,
        in_specs=specs,
        out_specs=[VMEM] * len(out_shape),
        scratch_shapes=list(scratch),
        compiler_params=pltpu.CompilerParams(vmem_limit_bytes=48 * 2**20),
        cost_estimate=pl.CostEstimate(flops=flops, bytes_accessed=moved, transcendentals=0),
    )(*args)


def is_top():
    return lax.axis_index("section") == lax.axis_size("section") - 1


def dp_bit(n):
    return lax.rem(lax.div(lax.axis_index("dp"), 1 << n), 2)


def like(shape, dtype):
    return jax.ShapeDtypeStruct(shape, dtype)


def put_taps(values, taps, bins, dilation, orientation):
    rows, cols = values.shape
    place = lax.broadcasted_iota(jnp.int32, (bins, cols), 0)
    taps[:, cols : 2 * cols] = values
    for b in range(rows // bins):
        at = slice(b * bins, (b + 1) * bins)
        group = values[at].astype(F32)
        later = pltpu.roll(group, bins - dilation, 0)
        later = jnp.where(place < bins - dilation, later, 0.0).astype(BF16)
        earlier = pltpu.roll(group, dilation, 0)
        earlier = jnp.where(place >= dilation, earlier, 0.0).astype(BF16)
        first, third = (earlier, later) if orientation == 1 else (later, earlier)
        taps[at, 0:cols] = first
        taps[at, 2 * cols : 3 * cols] = third


def back_product(taps, weight, cols):
    total = None
    for k in range(3):
        part = lax.dot_general(
            taps[:, k * cols : (k + 1) * cols], weight[k], NT, preferred_element_type=F32
        )
        total = part if total is None else total + part
    return total


def forward(mixed, at, taps, bins, dilation, weight, slope):
    put_taps(mixed[at, :], taps, bins, dilation, 1)
    flat = weight[...].reshape(-1, weight.shape[2])
    y = jnp.dot(taps[...], flat, preferred_element_type=F32)
    gate = jax.nn.sigmoid(y)
    slope[...] = gate * (1.0 + y * (1.0 - gate))


def backward(g, taps, bins, dilation, slope):
    delta = (g * slope[...]).astype(BF16)
    put_taps(delta, taps, bins, dilation, -1)


def below_of(g, taps, weight, col, out):
    cols = slice(col, col + out.shape[1])
    dh = back_product(taps, weight[:, cols, :], weight.shape[2])
    out[...] = (g[:, cols].astype(F32) + dh).astype(BF16)


def first_kernel(dil, ts, x, table, weight, top, mixed, weight_v, top_v, hot, slope, taps, g_out, *s):
    ts_s, x_v, table_v, tab, forward_taps, sems = s
    pairs = ((ts, ts_s), (x, x_v), (table, table_v), (weight, weight_v), (top, top_v))
    copies = [pltpu.make_async_copy(a, b, sems.at[n]) for n, (a, b) in enumerate(pairs)]
    for copy in copies:
        copy.start()
    groups, bins, chans = x.shape
    for copy in copies[:3]:
        copy.wait()
    tab[...] = table_v[...].astype(F32)
    for b in range(groups):
        row = x_v[b].astype(F32) + tab[pl.ds(ts_s[b], 1), :]
        mixed[b * bins : (b + 1) * bins, :] = row.astype(BF16)
    steps = lax.broadcasted_iota(jnp.int32, hot.shape, 0)
    lanes = lax.broadcasted_iota(jnp.int32, hot.shape, 1)
    marks = jnp.zeros(hot.shape, F32)
    for b in range(groups):
        marks = jnp.where((lanes == b) & (steps == ts_s[b]), 1.0, marks)
    hot[...] = marks
    copies[3].wait()
    rows = slope.shape[0]
    forward(mixed, slice(0, rows), forward_taps, bins, dil[0], weight_v, slope)
    copies[4].wait()
    g = top_v[...].reshape(groups * bins, chans)[0:rows]
    backward(g.astype(F32), taps, bins, dil[0], slope)
    below_of(g, taps, weight_v, 0, g_out)


def other_kernel(start, bins, dil, mixed, weight, top, slope, taps, g_out, forward_taps):
    at = slice(start, start + slope.shape[0])
    forward(mixed, at, forward_taps, bins, dil[0], weight, slope)
    g = top[...].reshape(mixed.shape)[at]
    backward(g.astype(F32), taps, bins, dil[0], slope)
    below_of(g, taps, weight, 0, g_out)


def rest_kernel(col, weight, top, *rest):
    taps, g_out = rest[:-1], rest[-1]
    part = taps[0].shape[0]
    g = top[...].reshape(-1, top.shape[2])
    for n, ref in enumerate(taps):
        at = slice(n * part, (n + 1) * part)
        below_of(g[at], ref, weight, col, g_out.at[at])


def turn_kernel(mixed, h_t):
    h_t[...] = mixed[...].T


def layer_kernel(start, bins, dil, slope, weight, top, *rest):
    early, late, out, out_late, taps = rest
    rows = slope.shape[0]
    got = jnp.concatenate([early[...], late[start : start + rows]], axis=1)
    fresh = top[...].reshape(-1, top.shape[2])[start : start + rows]
    g = jnp.where(is_top(), fresh.astype(F32), got.astype(F32))
    backward(g, taps, bins, dil[0], slope)
    below_of(g, taps, weight, 0, out)
    below_of(g, taps, weight, out.shape[1], out_late)


def upstream(col, top, recv):
    got = [ref[...].astype(F32) for ref in recv]
    got = got[0] if len(got) == 1 else jnp.concatenate(got, axis=0)
    rows, width = got.shape
    fresh = top[...].reshape(rows, top.shape[-1])[:, col : col + width]
    return jnp.where(is_top(), fresh.astype(F32), got)


def delta_of(g, slope, col):
    width = g.shape[1]
    factor = jnp.concatenate([ref[:, col : col + width] for ref in slope], axis=0)
    return (g * factor).astype(BF16)


def round_bit(orders, n, other=0):
    mine, theirs = dp_bit(orders[other][n]), dp_bit(orders[1 - other][n])
    return jnp.where(dp_bit(0) == 0, mine, theirs)


def weight_blocks(h_t, taps, scale, keep, send, cols):
    half = h_t.shape[0] // 2
    bit = dp_bit(0)
    for ref, part in ((keep, bit), (send, 1 - bit)):
        left = h_t[pl.ds(pl.multiple_of(part * half, half), half), :]
        prod = jnp.dot(left, taps[...], preferred_element_type=F32)
        ref[:, 0:cols] = (prod * scale).astype(BF16)


def weight_kernel(col, scale, dil, top, h_t, *rest):
    slope, recv, out = rest[:PARTS], rest[PARTS:-4], rest[-4:]
    g_used, taps, keep, send = out
    width = g_used.shape[1]
    g = upstream(col, top, recv)
    g_used[...] = g.astype(BF16)
    delta = delta_of(g, slope, col)
    put_taps(delta, taps, top.shape[1], dil[0], -1)
    weight_blocks(h_t, taps, scale, keep, send, 3 * width)


def back_kernel(col, taps, weight, acc):
    width = taps.shape[1] // 3
    acc[...] = back_product(taps, weight[:, :, col : col + width], width)


def last_kernel(col, scale, prior, dil, top, h_t, weight, hot, *rest):
    slope, recv = rest[:PARTS], rest[PARTS : -4 - 2 * prior]
    g_prior, acc = rest[-4 - 2 * prior : -4 - prior], rest[-4 - prior : -4]
    keep, send, grad, taps = rest[-4:]
    groups, bins, chans = grad.shape
    width = taps.shape[1] // 3
    g = upstream(col, top, recv)
    delta = delta_of(g, slope, col)
    put_taps(delta, taps, bins, dil[0], -1)
    dh = back_product(taps, weight[:, :, col : col + width], width)
    for ref in acc:
        dh = dh + ref[...]
    whole = jnp.concatenate([ref[...].astype(F32) for ref in g_prior] + [g], axis=1)
    grad[...] = (whole + dh).astype(BF16).reshape(groups, bins, chans)
    table = jnp.zeros((hot.shape[0], chans), F32)
    for b in range(groups):
        total = jnp.sum(dh[b * bins : (b + 1) * bins], axis=0, keepdims=True)
        table = table + hot[:, b : b + 1] * (total * scale)
    table_t = table.T.astype(BF16)
    weight_blocks(h_t, taps, scale, keep, send, 3 * width)
    half = chans // 2
    bit = dp_bit(0)
    for ref, part in ((send, 1 - bit), (keep, bit)):
        ref[:, 3 * width :] = jnp.where(part == 0, table_t[0:half], table_t[half:])


def fold_kernel(orders, n, keep, recv, keep_out, send_out):
    size = keep_out.shape[0]
    bit = round_bit(orders, n)
    for ref, part in ((keep_out, bit), (send_out, 1 - bit)):
        at = pl.ds(pl.multiple_of(part * size, size), size)
        ref[...] = (keep[at, :].astype(F32) + recv[at, :].astype(F32)).astype(BF16)


def assemble_kernel(orders, widths, lists, *refs):
    weight_out, table_out, table_t = refs[-3:]
    pieces = list(refs[:-3])
    col = 0
    for width in widths:
        for offsets in lists:
            ref = pieces.pop(0)
            size = ref.shape[0] // len(offsets)
            for slot, (core, flips) in enumerate(offsets):
                block = dp_bit(0) if core == 0 else 1 - dp_bit(0)
                for n in range(len(orders[0])):
                    bit = round_bit(orders, n, core)
                    block = block * 2 + (1 - bit if (flips >> n) & 1 else bit)
                row = pl.ds(pl.multiple_of(block * size, size), size)
                here = slice(slot * size, (slot + 1) * size)
                for k in range(3):
                    weight_out[k, row, col : col + width] = ref[here, k * width : (k + 1) * width]
                if ref.shape[1] > 3 * width:
                    table_t[row, :] = ref[here, 3 * width :].astype(F32)
        col += width
    table_out[...] = table_t[...].T[: table_out.shape[0]].astype(BF16)


def swap(value, bit, other=None):
    count = lax.axis_size("dp")
    bits = (bit, bit if other is None else other)
    return lax.ppermute(value, "dp", [(i, i ^ (1 << bits[i % 2])) for i in range(count)])


def body(section_input, top_grad, conv_weight, step_table, timesteps, dilations):
    section_count = lax.axis_size("section")
    dp_count = lax.axis_size("dp")
    dp_bits = dp_count.bit_length() - 1
    x = section_input[0]
    weight = conv_weight[0]
    table = step_table[0]
    groups, bins, chans = x.shape
    rows = groups * bins
    sent = SENT
    scale = 1.0 / math.sqrt(groups * dp_count * bins)
    unit = 2 * rows * chans * chans * 3
    starts = [sum(sent[:n]) for n in range(len(sent))]

    part = rows // PARTS
    room = pltpu.VMEM((part, 3 * chans), BF16)
    of_part = [
        like((part, chans), F32),
        like((part, 3 * chans), BF16),
        like((part, sent[0]), BF16),
    ]
    far = (timesteps, x, table, weight, top_grad)
    mixed, weight, top, hot, *first = call(
        first_kernel,
        [
            like((rows, chans), BF16),
            like(weight.shape, BF16),
            like(x.shape, BF16),
            like((128, 128), F32),
        ]
        + of_part,
        (dilations,) + tuple(pltpu.with_memory_space_constraint(v, pltpu.HBM) for v in far),
        smem=1,
        far=5,
        scratch=[
            pltpu.SMEM(timesteps.shape, jnp.int32),
            pltpu.VMEM(x.shape, BF16),
            pltpu.VMEM(table.shape, BF16),
            pltpu.VMEM(table.shape, F32),
            room,
            pltpu.SemaphoreType.DMA((5,)),
        ],
        flops=2 * unit // PARTS,
    )

    def below(value):
        return lax.ppermute(value, "section", [(i, i - 1) for i in range(1, section_count)])

    made = [first]
    for n in range(1, PARTS):
        made.append(
            call(
                functools.partial(other_kernel, n * part, bins),
                of_part,
                (dilations, mixed, weight, top),
                smem=1,
                scratch=[room],
                flops=2 * unit // PARTS,
            )
        )
    slope = [v[0] for v in made]
    late = call(
        functools.partial(rest_kernel, sent[0]),
        [like((rows, sent[1]), BF16)],
        (weight, top) + tuple(v[1] for v in made),
        flops=unit // 2,
    )[0]
    got = [[below(v[2]) for v in made], [below(late)]]
    h_t = call(turn_kernel, [like((chans, rows), BF16)], (mixed,), flops=unit // 9)[0]
    for _ in range(section_count - 2):
        pieces = [
            call(
                functools.partial(layer_kernel, n * part, bins),
                [like((part, cols), BF16) for cols in sent],
                (dilations, slope[n], weight, top, got[0][n], got[1][0]),
                smem=1,
                scratch=[room],
                flops=unit // PARTS,
            )
            for n in range(PARTS)
        ]
        late = jnp.concatenate([v[1] for v in pieces], axis=0)
        got = [[below(v[0]) for v in pieces], [below(late)]]

    inner = list(range(1, dp_bits - 1))
    orders = (inner, inner[::-1])
    chains = []
    used = []
    accs = []
    for n, width in enumerate(sent):
        col = starts[n]
        recv = tuple(slope) + tuple(got[n])
        if n < len(sent) - 1:
            g_now, taps_now, *blocks = call(
                functools.partial(weight_kernel, col, scale),
                [like((rows, width), BF16), like((rows, 3 * width), BF16)]
                + [like((chans // 2, 3 * width), BF16)] * 2,
                (dilations, top, h_t) + recv,
                smem=1,
                    flops=unit * width // chans,
            )
            acc = call(
                functools.partial(back_kernel, col),
                [like((rows, chans), F32)],
                (taps_now, weight),
                flops=10**11,
            )[0]
            used.append(g_now)
            accs.append(acc)
        else:
            *blocks, grad = call(
                functools.partial(last_kernel, col, scale, len(used)),
                [like((chans // 2, 3 * width + 128), BF16)] * 2 + [like(x.shape, BF16)],
                (dilations, top, h_t, weight, hot) + recv + tuple(used) + tuple(accs),
                smem=1,
                    scratch=[pltpu.VMEM((rows, 3 * width), BF16)],
                flops=10**11,
            )
        chains.append((width, blocks))

    widths = []
    pieces = []
    before = []
    for width, (keep, send) in chains:
        rounds = []

        def ordered(arrived):
            rounds.append(arrived)
            if len(rounds) < len(before):
                arrived = lax.optimization_barrier((arrived, before[len(rounds)]))[0]
            return arrived

        if before:
            send = lax.optimization_barrier((send, before[1]))[0]
        recv = ordered(swap(send, 0))
        for n in range(len(inner)):
            half = [like((keep.shape[0] // 2, keep.shape[1]), BF16)] * 2
            keep, send = call(functools.partial(fold_kernel, orders, n), half, (keep, recv))
            recv = ordered(swap(send, orders[0][n], orders[1][n]))
        keep = (keep.astype(F32) + recv.astype(F32)).astype(BF16)
        own = (keep.astype(F32) + ordered(swap(keep, dp_bits - 1)).astype(F32)).astype(BF16)
        held = [(own, [(0, 0)])]
        for n in reversed(range(len(inner))):
            message = jnp.concatenate([v for v, _ in held], axis=0) if len(held) > 1 else own
            flips = [(0, f ^ (1 << n)) for _, offs in held for _, f in offs]
            held.append((ordered(swap(message, orders[0][n], orders[1][n])), flips))
        early = jnp.concatenate([v for v, _ in held[:-1]], axis=0)
        held.append((swap(early, 0), [(1, f) for _, offs in held[:-1] for _, f in offs]))
        held.append((swap(held[-2][0], 0), [(1, f) for _, f in held[-2][1]]))
        pieces += [v for v, _ in held]
        widths.append(width)
        before = rounds

    weight_out, table_out = call(
        functools.partial(assemble_kernel, orders, widths, [o for _, o in held]),
        [like(weight.shape, BF16), like(table.shape, BF16)],
        tuple(pieces),
        scratch=[pltpu.VMEM((chans, 128), F32)],
    )
    return (grad[None], weight_out[None], table_out[None])


def solution(mesh):
    placed = (
        P("section", "dp", None, None),
        P("dp", None, None),
        P("section", None, None, None),
        P("section", None, None),
        P("dp"),
        P("section"),
    )
    return jax.shard_map(
        body,
        mesh=mesh,
        in_specs=placed,
        out_specs=(
            P("section", "dp", None, None),
            P("section", None, None, None),
            P("section", None, None),
        ),
        check_vma=False,
    )
```

```python
import functools
import math

import jax
import jax.numpy as jnp
from jax import lax
from jax.experimental import pallas as pl
from jax.experimental.pallas import tpu as pltpu
from jax.sharding import PartitionSpec as P

SENT = (256, 256)
PARTS = 2
F32 = jnp.float32
BF16 = jnp.bfloat16
VMEM = pl.BlockSpec(memory_space=pltpu.VMEM)
SMEM = pl.BlockSpec(memory_space=pltpu.SMEM)
HBM = pl.BlockSpec(memory_space=pltpu.HBM)
NT = (((1,), (1,)), ((), ()))


def call(kernel, out_shape, args, smem=0, far=0, scratch=(), flops=0):
    specs = [SMEM] * smem + [HBM] * far + [VMEM] * (len(args) - smem - far)
    moved = sum(a.size * a.dtype.itemsize for a in args)
    moved += sum(math.prod(o.shape) * o.dtype.itemsize for o in out_shape)
    return pl.pallas_call(
        kernel,
        out_shape=out_shape,
        in_specs=specs,
        out_specs=[VMEM] * len(out_shape),
        scratch_shapes=list(scratch),
        compiler_params=pltpu.CompilerParams(vmem_limit_bytes=48 * 2**20),
        cost_estimate=pl.CostEstimate(flops=flops, bytes_accessed=moved, transcendentals=0),
    )(*args)


def is_top():
    return lax.axis_index("section") == lax.axis_size("section") - 1


def dp_bit(n):
    return lax.rem(lax.div(lax.axis_index("dp"), 1 << n), 2)


def like(shape, dtype):
    return jax.ShapeDtypeStruct(shape, dtype)


def put_taps(values, taps, bins, dilation, orientation):
    rows, cols = values.shape
    place = lax.broadcasted_iota(jnp.int32, (bins, cols), 0)
    taps[:, cols : 2 * cols] = values
    for b in range(rows // bins):
        at = slice(b * bins, (b + 1) * bins)
        group = values[at].astype(F32)
        later = pltpu.roll(group, bins - dilation, 0)
        later = jnp.where(place < bins - dilation, later, 0.0).astype(BF16)
        earlier = pltpu.roll(group, dilation, 0)
        earlier = jnp.where(place >= dilation, earlier, 0.0).astype(BF16)
        first, third = (earlier, later) if orientation == 1 else (later, earlier)
        taps[at, 0:cols] = first
        taps[at, 2 * cols : 3 * cols] = third


def back_product(taps, weight, cols):
    total = None
    for k in range(3):
        part = lax.dot_general(
            taps[:, k * cols : (k + 1) * cols], weight[k], NT, preferred_element_type=F32
        )
        total = part if total is None else total + part
    return total


def forward(mixed, at, taps, bins, dilation, weight, slope):
    put_taps(mixed[at, :], taps, bins, dilation, 1)
    flat = weight[...].reshape(-1, weight.shape[2])
    y = jnp.dot(taps[...], flat, preferred_element_type=F32)
    gate = jax.nn.sigmoid(y)
    slope[...] = gate * (1.0 + y * (1.0 - gate))


def backward(g, taps, bins, dilation, slope):
    delta = (g * slope[...]).astype(BF16)
    put_taps(delta, taps, bins, dilation, -1)


def below_of(g, taps, weight, col, out):
    cols = slice(col, col + out.shape[1])
    dh = back_product(taps, weight[:, cols, :], weight.shape[2])
    out[...] = (g[:, cols].astype(F32) + dh).astype(BF16)


def first_kernel(dil, ts, x, table, weight, top, mixed, weight_v, top_v, hot, slope, taps, g_out, *s):
    ts_s, x_v, table_v, tab, forward_taps, sems = s
    pairs = ((ts, ts_s), (x, x_v), (table, table_v), (weight, weight_v), (top, top_v))
    copies = [pltpu.make_async_copy(a, b, sems.at[n]) for n, (a, b) in enumerate(pairs)]
    for copy in copies:
        copy.start()
    groups, bins, chans = x.shape
    for copy in copies[:3]:
        copy.wait()
    tab[...] = table_v[...].astype(F32)
    for b in range(groups):
        row = x_v[b].astype(F32) + tab[pl.ds(ts_s[b], 1), :]
        mixed[b * bins : (b + 1) * bins, :] = row.astype(BF16)
    steps = lax.broadcasted_iota(jnp.int32, hot.shape, 0)
    lanes = lax.broadcasted_iota(jnp.int32, hot.shape, 1)
    marks = jnp.zeros(hot.shape, F32)
    for b in range(groups):
        marks = jnp.where((lanes == b) & (steps == ts_s[b]), 1.0, marks)
    hot[...] = marks
    copies[3].wait()
    rows = slope.shape[0]
    forward(mixed, slice(0, rows), forward_taps, bins, dil[0], weight_v, slope)
    copies[4].wait()
    g = top_v[...].reshape(groups * bins, chans)[0:rows]
    backward(g.astype(F32), taps, bins, dil[0], slope)
    below_of(g, taps, weight_v, 0, g_out)


def other_kernel(start, bins, dil, mixed, weight, top, slope, taps, g_out, forward_taps):
    at = slice(start, start + slope.shape[0])
    forward(mixed, at, forward_taps, bins, dil[0], weight, slope)
    g = top[...].reshape(mixed.shape)[at]
    backward(g.astype(F32), taps, bins, dil[0], slope)
    below_of(g, taps, weight, 0, g_out)


def rest_kernel(col, weight, top, *rest):
    taps, g_out = rest[:-1], rest[-1]
    part = taps[0].shape[0]
    g = top[...].reshape(-1, top.shape[2])
    for n, ref in enumerate(taps):
        at = slice(n * part, (n + 1) * part)
        below_of(g[at], ref, weight, col, g_out.at[at])


def turn_kernel(mixed, h_t):
    h_t[...] = mixed[...].T


def layer_kernel(start, bins, dil, slope, weight, top, *rest):
    early, late, out, out_late, taps = rest
    rows = slope.shape[0]
    got = jnp.concatenate([early[...], late[start : start + rows]], axis=1)
    fresh = top[...].reshape(-1, top.shape[2])[start : start + rows]
    g = jnp.where(is_top(), fresh.astype(F32), got.astype(F32))
    backward(g, taps, bins, dil[0], slope)
    below_of(g, taps, weight, 0, out)
    below_of(g, taps, weight, out.shape[1], out_late)


def upstream(col, top, recv):
    got = [ref[...].astype(F32) for ref in recv]
    got = got[0] if len(got) == 1 else jnp.concatenate(got, axis=0)
    rows, width = got.shape
    fresh = top[...].reshape(rows, top.shape[-1])[:, col : col + width]
    return jnp.where(is_top(), fresh.astype(F32), got)


def delta_of(g, slope, col):
    width = g.shape[1]
    factor = jnp.concatenate([ref[:, col : col + width] for ref in slope], axis=0)
    return (g * factor).astype(BF16)


def by_core(even, odd, other=False):
    return jnp.where(dp_bit(0) == (1 if other else 0), even, odd)


def place_in(bits, mask=0):
    place = 0
    for n in reversed(bits):
        place = place * 2 + (1 - dp_bit(n) if (mask >> n) & 1 else dp_bit(n))
    return place


def mask_of(bits, offset):
    return sum(1 << n for j, n in enumerate(bits) if (offset >> j) & 1)


def weight_blocks(h_t, taps, scale, keep, send, cols):
    half = h_t.shape[0] // 2
    bit = dp_bit(0)
    for ref, part in ((keep, bit), (send, 1 - bit)):
        left = h_t[pl.ds(pl.multiple_of(part * half, half), half), :]
        prod = jnp.dot(left, taps[...], preferred_element_type=F32)
        ref[:, 0:cols] = (prod * scale).astype(BF16)


def weight_kernel(col, scale, dil, top, h_t, *rest):
    slope, recv, out = rest[:PARTS], rest[PARTS:-4], rest[-4:]
    g_used, taps, keep, send = out
    width = g_used.shape[1]
    g = upstream(col, top, recv)
    g_used[...] = g.astype(BF16)
    delta = delta_of(g, slope, col)
    put_taps(delta, taps, top.shape[1], dil[0], -1)
    weight_blocks(h_t, taps, scale, keep, send, 3 * width)


def back_kernel(col, taps, weight, acc):
    width = taps.shape[1] // 3
    acc[...] = back_product(taps, weight[:, :, col : col + width], width)


def last_kernel(col, scale, prior, dil, top, h_t, weight, hot, *rest):
    slope, recv = rest[:PARTS], rest[PARTS : -4 - 2 * prior]
    g_prior, acc = rest[-4 - 2 * prior : -4 - prior], rest[-4 - prior : -4]
    keep, send, grad, taps = rest[-4:]
    groups, bins, chans = grad.shape
    width = taps.shape[1] // 3
    g = upstream(col, top, recv)
    delta = delta_of(g, slope, col)
    put_taps(delta, taps, bins, dil[0], -1)
    dh = back_product(taps, weight[:, :, col : col + width], width)
    for ref in acc:
        dh = dh + ref[...]
    whole = jnp.concatenate([ref[...].astype(F32) for ref in g_prior] + [g], axis=1)
    grad[...] = (whole + dh).astype(BF16).reshape(groups, bins, chans)
    table = jnp.zeros((hot.shape[0], chans), F32)
    for b in range(groups):
        total = jnp.sum(dh[b * bins : (b + 1) * bins], axis=0, keepdims=True)
        table = table + hot[:, b : b + 1] * (total * scale)
    table_t = table.T.astype(BF16)
    weight_blocks(h_t, taps, scale, keep, send, 3 * width)
    half = chans // 2
    bit = dp_bit(0)
    for ref, part in ((send, 1 - bit), (keep, bit)):
        ref[:, 3 * width :] = jnp.where(part == 0, table_t[0:half], table_t[half:])


def fold_kernel(level, count, *refs):
    summands, out = refs[:count], refs[count:]
    size = out[0].shape[0]
    for offset, ref in enumerate(out):
        part = by_core(*(place_in(bits, mask_of(bits, offset)) for bits in level))
        at = pl.ds(pl.multiple_of(part * size, size), size)
        total = summands[0][at, :].astype(F32)
        for other in summands[1:]:
            total = total + other[at, :].astype(F32)
        ref[...] = total.astype(BF16)


def assemble_kernel(plans, *refs):
    weight_out, table_out, table_t = refs[-3:]
    pieces = list(refs[:-3])
    col = 0
    for width, levels, lists in plans:
        for offsets in lists:
            ref = pieces.pop(0)
            size = ref.shape[0] // len(offsets)
            for slot, (core, masks) in enumerate(offsets):
                blocks = []
                for parity in (0, 1):
                    block = 0
                    for level in levels:
                        bits = level[parity]
                        block = block * (1 << len(bits)) + place_in(bits, masks[parity])
                    blocks.append(block)
                block = by_core(*blocks, other=core == 1)
                half = dp_bit(0) if core == 0 else 1 - dp_bit(0)
                block = block + half * (weight_out.shape[1] // 2 // size)
                row = pl.ds(pl.multiple_of(block * size, size), size)
                here = slice(slot * size, (slot + 1) * size)
                for k in range(3):
                    weight_out[k, row, col : col + width] = ref[here, k * width : (k + 1) * width]
                if ref.shape[1] > 3 * width:
                    table_t[row, :] = ref[here, 3 * width :].astype(F32)
        col += width
    table_out[...] = table_t[...].T[: table_out.shape[0]].astype(BF16)


def swap(value, even, odd=None):
    count = lax.axis_size("dp")
    masks = (even, even if odd is None else odd)
    return lax.ppermute(value, "dp", [(i, i ^ masks[i % 2]) for i in range(count)])


def single(bits):
    return [((a,), (b,)) for a, b in zip(bits, reversed(bits))]


def double(bits):
    pairs = [tuple(bits[n : n + 2]) for n in range(0, len(bits), 2)]
    return [(pair, pair) for pair in pairs]


def offsets_in(level):
    return range(1, 1 << len(level[0]))


def body(section_input, top_grad, conv_weight, step_table, timesteps, dilations):
    section_count = lax.axis_size("section")
    dp_count = lax.axis_size("dp")
    dp_bits = dp_count.bit_length() - 1
    x = section_input[0]
    weight = conv_weight[0]
    table = step_table[0]
    groups, bins, chans = x.shape
    rows = groups * bins
    sent = SENT
    scale = 1.0 / math.sqrt(groups * dp_count * bins)
    unit = 2 * rows * chans * chans * 3
    starts = [sum(sent[:n]) for n in range(len(sent))]

    part = rows // PARTS
    room = pltpu.VMEM((part, 3 * chans), BF16)
    of_part = [
        like((part, chans), F32),
        like((part, 3 * chans), BF16),
        like((part, sent[0]), BF16),
    ]
    far = (timesteps, x, table, weight, top_grad)
    mixed, weight, top, hot, *first = call(
        first_kernel,
        [
            like((rows, chans), BF16),
            like(weight.shape, BF16),
            like(x.shape, BF16),
            like((128, 128), F32),
        ]
        + of_part,
        (dilations,) + tuple(pltpu.with_memory_space_constraint(v, pltpu.HBM) for v in far),
        smem=1,
        far=5,
        scratch=[
            pltpu.SMEM(timesteps.shape, jnp.int32),
            pltpu.VMEM(x.shape, BF16),
            pltpu.VMEM(table.shape, BF16),
            pltpu.VMEM(table.shape, F32),
            room,
            pltpu.SemaphoreType.DMA((5,)),
        ],
        flops=2 * unit // PARTS,
    )

    def below(value):
        return lax.ppermute(value, "section", [(i, i - 1) for i in range(1, section_count)])

    made = [first]
    for n in range(1, PARTS):
        made.append(
            call(
                functools.partial(other_kernel, n * part, bins),
                of_part,
                (dilations, mixed, weight, top),
                smem=1,
                scratch=[room],
                flops=2 * unit // PARTS,
            )
        )
    slope = [v[0] for v in made]
    late = call(
        functools.partial(rest_kernel, sent[0]),
        [like((rows, sent[1]), BF16)],
        (weight, top) + tuple(v[1] for v in made),
        flops=unit // 2,
    )[0]
    got = [[below(v[2]) for v in made], [below(late)]]
    h_t = call(turn_kernel, [like((chans, rows), BF16)], (mixed,), flops=unit // 9)[0]
    for _ in range(section_count - 2):
        pieces = [
            call(
                functools.partial(layer_kernel, n * part, bins),
                [like((part, cols), BF16) for cols in sent],
                (dilations, slope[n], weight, top, got[0][n], got[1][0]),
                smem=1,
                scratch=[room],
                flops=unit // PARTS,
            )
            for n in range(PARTS)
        ]
        late = jnp.concatenate([v[1] for v in pieces], axis=0)
        got = [[below(v[0]) for v in pieces], [below(late)]]

    inner = list(range(1, dp_bits - 1))
    plans = []
    pieces = []
    before = []
    ahead = None
    used = []
    accs = []
    for n, width in enumerate(sent):
        col = starts[n]
        if ahead is not None and HOLD:
            got[n], _ = lax.optimization_barrier((got[n], ahead))
        recv = tuple(slope) + tuple(got[n])
        if n < len(sent) - 1:
            g_now, taps_now, *blocks = call(
                functools.partial(weight_kernel, col, scale),
                [like((rows, width), BF16), like((rows, 3 * width), BF16)]
                + [like((chans // 2, 3 * width), BF16)] * 2,
                (dilations, top, h_t) + recv,
                smem=1,
                    flops=unit * width // chans,
            )
            acc = call(
                functools.partial(back_kernel, col),
                [like((rows, chans), F32)],
                (taps_now, weight),
                flops=10**11,
            )[0]
            used.append(g_now)
            accs.append(acc)
        else:
            *blocks, grad = call(
                functools.partial(last_kernel, col, scale, len(used)),
                [like((chans // 2, 3 * width + 128), BF16)] * 2 + [like(x.shape, BF16)],
                (dilations, top, h_t, weight, hot) + recv + tuple(used) + tuple(accs),
                smem=1,
                    scratch=[pltpu.VMEM((rows, 3 * width), BF16)],
                flops=10**11,
            )
        reduce_by, gather_by = CHAINS[n]
        levels = reduce_by(inner)
        rounds = []

        def ordered(*arrived):
            arrived = list(arrived)
            at = TIES.get(len(rounds))
            rounds.append(arrived)
            if before and at is not None:
                arrived = list(lax.optimization_barrier((*arrived, *before[at]))[: len(arrived)])
            return arrived

        if before and FIRST:
            blocks[1] = lax.optimization_barrier((blocks[1], *before[1]))[0]
        blocks = [blocks[0]] + ordered(swap(blocks[1], 1))
        for level in levels:
            split = 1 << len(level[0])
            blocks = call(
                functools.partial(fold_kernel, level, len(blocks)),
                [like((blocks[0].shape[0] // split, blocks[0].shape[1]), BF16)] * split,
                tuple(blocks),
            )
            ahead = blocks[1]
            arrived = [
                swap(blocks[o], *(mask_of(bits, o) for bits in level)) for o in offsets_in(level)
            ]
            blocks = [blocks[0]] + ordered(*arrived)
        keep = sum(v.astype(F32) for v in blocks).astype(BF16)
        arrived = ordered(swap(keep, 1 << (dp_bits - 1)))
        own = (keep.astype(F32) + arrived[0].astype(F32)).astype(BF16)
        held = [(own, [(0, (0, 0))])]
        for level in reversed(gather_by(inner)):
            message = jnp.concatenate([v for v, _ in held], axis=0) if len(held) > 1 else own
            offsets = [m for _, offs in held for _, m in offs]
            masks = [tuple(mask_of(bits, o) for bits in level) for o in offsets_in(level)]
            arrived = ordered(*(swap(message, *mask) for mask in masks))
            held += [
                (v, [(0, (m[0] ^ e, m[1] ^ o)) for m in offsets]) for v, (e, o) in zip(arrived, masks)
            ]
        late = 1 if gather_by is single else 3
        early = jnp.concatenate([v for v, _ in held[:-late]], axis=0) if len(held) > late + 1 else held[0][0]
        late = jnp.concatenate([v for v, _ in held[-late:]], axis=0) if late > 1 else held[-1][0]
        count = early.shape[0] // own.shape[0]
        masks = [m for _, offs in held for _, m in offs]
        arrived = ordered(swap(early, 1), swap(late, 1))
        held.append((arrived[0], [(1, m) for m in masks[:count]]))
        held.append((arrived[1], [(1, m) for m in masks[count:]]))
        pieces += [v for v, _ in held]
        plans.append((width, levels, [offs for _, offs in held]))
        before = rounds

    weight_out, table_out = call(
        functools.partial(assemble_kernel, plans),
        [like(weight.shape, BF16), like(table.shape, BF16)],
        tuple(pieces),
        scratch=[pltpu.VMEM((chans, 128), F32)],
    )
    return (grad[None], weight_out[None], table_out[None])


CHAINS = ((single, single), (single, double))
TIES = {4: 5}
FIRST = True
HOLD = False


def solution(mesh):
    placed = (
        P("section", "dp", None, None),
        P("dp", None, None),
        P("section", None, None, None),
        P("section", None, None),
        P("dp"),
        P("section"),
    )
    return jax.shard_map(
        body,
        mesh=mesh,
        in_specs=placed,
        out_specs=(
            P("section", "dp", None, None),
            P("section", None, None, None),
            P("section", None, None),
        ),
        check_vma=False,
    )
```

```python
import functools
import math

import jax
import jax.numpy as jnp
from jax import lax
from jax.experimental import pallas as pl
from jax.experimental.pallas import tpu as pltpu
from jax.sharding import PartitionSpec as P

SENT = (256, 256)
PARTS = 2
F32 = jnp.float32
BF16 = jnp.bfloat16
VMEM = pl.BlockSpec(memory_space=pltpu.VMEM)
SMEM = pl.BlockSpec(memory_space=pltpu.SMEM)
HBM = pl.BlockSpec(memory_space=pltpu.HBM)
NT = (((1,), (1,)), ((), ()))


def call(kernel, out_shape, args, smem=0, far=0, scratch=(), flops=0):
    specs = [SMEM] * smem + [HBM] * far + [VMEM] * (len(args) - smem - far)
    moved = sum(a.size * a.dtype.itemsize for a in args)
    moved += sum(math.prod(o.shape) * o.dtype.itemsize for o in out_shape)
    return pl.pallas_call(
        kernel,
        out_shape=out_shape,
        in_specs=specs,
        out_specs=[VMEM] * len(out_shape),
        scratch_shapes=list(scratch),
        compiler_params=pltpu.CompilerParams(vmem_limit_bytes=32 * 2**20),
        cost_estimate=pl.CostEstimate(flops=flops, bytes_accessed=moved, transcendentals=0),
    )(*args)


def is_top():
    return lax.axis_index("section") == lax.axis_size("section") - 1


def dp_bit(n):
    return lax.rem(lax.div(lax.axis_index("dp"), 1 << n), 2)


def like(shape, dtype):
    return jax.ShapeDtypeStruct(shape, dtype)


def shift_matrix(bins, dilation):
    row = lax.broadcasted_iota(jnp.int32, (bins, bins), 0)
    col = lax.broadcasted_iota(jnp.int32, (bins, bins), 1)
    both = [jnp.where(col == row + by, 1.0, 0.0).astype(BF16) for by in (-dilation, dilation)]
    return jnp.concatenate(both, axis=0)


def put_taps(values, taps, shift, orientation):
    rows, cols = values.shape
    bins = shift.shape[1]
    taps[:, cols : 2 * cols] = values
    for b in range(rows // bins):
        at = slice(b * bins, (b + 1) * bins)
        moved = jnp.dot(shift[...], values[at], preferred_element_type=F32).astype(BF16)
        earlier, later = moved[:bins], moved[bins:]
        first, third = (earlier, later) if orientation == 1 else (later, earlier)
        taps[at, 0:cols] = first
        taps[at, 2 * cols : 3 * cols] = third


def back_product(taps, weight, cols):
    total = None
    for k in range(3):
        part = lax.dot_general(
            taps[:, k * cols : (k + 1) * cols], weight[k], NT, preferred_element_type=F32
        )
        total = part if total is None else total + part
    return total


def forward(h, taps, shift, weight, slope, wait=None):
    put_taps(h, taps, shift, 1)
    chans = h.shape[1]
    y = None
    for k in range(3):
        if wait is not None:
            wait(k)
        part = jnp.dot(taps[:, k * chans : (k + 1) * chans], weight[k], preferred_element_type=F32)
        y = part if y is None else y + part
    gate = jax.nn.sigmoid(y)
    slope[...] = gate * (1.0 + y * (1.0 - gate))


def backward(g, taps, shift, slope):
    delta = (g * slope[...]).astype(BF16)
    put_taps(delta, taps, shift, -1)


def below_of(g, taps, weight, col, out):
    cols = slice(col, col + out.shape[1])
    dh = back_product(taps, weight[:, cols, :], weight.shape[2])
    out[...] = (g[:, cols].astype(F32) + dh).astype(BF16)


def first_kernel(dil, ts, x, table, weight, top, mixed, weight_v, top_v, hot, shift, *rest):
    slope, taps, g_out, ts_s, x_v, table_v, tab, forward_taps, sems = rest
    groups, bins, chans = x.shape
    rows = slope.shape[0]
    near = slice(0, rows // bins)
    others = slice(rows // bins, groups)
    pairs = [(ts, ts_s), (table, table_v), (x.at[near], x_v.at[near])]
    pairs += [(weight.at[k], weight_v.at[k]) for k in range(3)]
    pairs += [(top.at[near], top_v.at[near]), (x.at[others], x_v.at[others]), (top.at[others], top_v.at[others])]
    copies = [pltpu.make_async_copy(a, b, sems.at[n]) for n, (a, b) in enumerate(pairs)]
    for copy in copies:
        copy.start()
    shift[...] = shift_matrix(bins, dil[0])
    for copy in copies[:3]:
        copy.wait()
    tab[...] = table_v[...].astype(F32)

    def mix(b):
        row = x_v[b].astype(F32) + tab[pl.ds(ts_s[b], 1), :]
        mixed[b * bins : (b + 1) * bins, :] = row.astype(BF16)

    for b in range(rows // bins):
        mix(b)
    forward(
        mixed[0:rows, :], forward_taps, shift, weight_v, slope, lambda k: copies[3 + k].wait()
    )
    copies[6].wait()
    g = top_v[near].reshape(rows, chans)
    backward(g.astype(F32), taps, shift, slope)
    below_of(g, taps, weight_v, 0, g_out)
    steps = lax.broadcasted_iota(jnp.int32, hot.shape, 0)
    lanes = lax.broadcasted_iota(jnp.int32, hot.shape, 1)
    marks = jnp.zeros(hot.shape, F32)
    for b in range(groups):
        marks = jnp.where((lanes == b) & (steps == ts_s[b]), 1.0, marks)
    hot[...] = marks
    copies[7].wait()
    for b in range(rows // bins, groups):
        mix(b)
    copies[8].wait()


def other_kernel(start, shift, mixed, weight, top, slope, taps, g_out, forward_taps):
    at = slice(start, start + slope.shape[0])
    forward(mixed[at, :], forward_taps, shift, weight, slope)
    g = top[...].reshape(mixed.shape)[at]
    backward(g.astype(F32), taps, shift, slope)
    below_of(g, taps, weight, 0, g_out)


def rest_kernel(col, weight, top, *rest):
    taps, g_out = rest[:-1], rest[-1]
    part = taps[0].shape[0]
    g = top[...].reshape(-1, top.shape[2])
    for n, ref in enumerate(taps):
        at = slice(n * part, (n + 1) * part)
        below_of(g[at], ref, weight, col, g_out.at[at])


def turn_kernel(mixed, h_t):
    h_t[...] = mixed[...].T


def layer_kernel(start, shift, slope, weight, top, *rest):
    early, late, out, out_late, taps = rest
    rows = slope.shape[0]
    got = jnp.concatenate([early[...], late[start : start + rows]], axis=1)
    fresh = top[...].reshape(-1, top.shape[2])[start : start + rows]
    g = jnp.where(is_top(), fresh.astype(F32), got.astype(F32))
    backward(g, taps, shift, slope)
    below_of(g, taps, weight, 0, out)
    below_of(g, taps, weight, out.shape[1], out_late)


def upstream(col, top, recv):
    got = [ref[...].astype(F32) for ref in recv]
    got = got[0] if len(got) == 1 else jnp.concatenate(got, axis=0)
    rows, width = got.shape
    fresh = top[...].reshape(rows, top.shape[-1])[:, col : col + width]
    return jnp.where(is_top(), fresh.astype(F32), got)


def delta_of(g, slope, col):
    width = g.shape[1]
    factor = jnp.concatenate([ref[:, col : col + width] for ref in slope], axis=0)
    return (g * factor).astype(BF16)


def by_core(even, odd, other=False):
    return jnp.where(dp_bit(0) == (1 if other else 0), even, odd)


def place_in(bits, mask=0):
    place = 0
    for n in reversed(bits):
        place = place * 2 + (1 - dp_bit(n) if (mask >> n) & 1 else dp_bit(n))
    return place


def mask_of(bits, offset):
    return sum(1 << n for j, n in enumerate(bits) if (offset >> j) & 1)


def weight_blocks(h_t, taps, scale, keep, send, cols):
    half = h_t.shape[0] // 2
    bit = dp_bit(0)
    for ref, part in ((keep, bit), (send, 1 - bit)):
        left = h_t[pl.ds(pl.multiple_of(part * half, half), half), :]
        prod = jnp.dot(left, taps[...], preferred_element_type=F32)
        ref[:, 0:cols] = (prod * scale).astype(BF16)


def weight_kernel(col, scale, shift, top, h_t, *rest):
    slope, recv, out = rest[:PARTS], rest[PARTS:-4], rest[-4:]
    g_used, taps, keep, send = out
    width = g_used.shape[1]
    g = upstream(col, top, recv)
    g_used[...] = g.astype(BF16)
    delta = delta_of(g, slope, col)
    put_taps(delta, taps, shift, -1)
    weight_blocks(h_t, taps, scale, keep, send, 3 * width)


def back_kernel(col, taps, weight, acc):
    width = taps.shape[1] // 3
    acc[...] = back_product(taps, weight[:, :, col : col + width], width)


def last_kernel(col, scale, prior, shift, top, h_t, weight, hot, *rest):
    slope, recv = rest[:PARTS], rest[PARTS : -4 - 2 * prior]
    g_prior, acc = rest[-4 - 2 * prior : -4 - prior], rest[-4 - prior : -4]
    keep, send, grad, taps = rest[-4:]
    groups, bins, chans = grad.shape
    width = taps.shape[1] // 3
    g = upstream(col, top, recv)
    delta = delta_of(g, slope, col)
    put_taps(delta, taps, shift, -1)
    dh = back_product(taps, weight[:, :, col : col + width], width)
    for ref in acc:
        dh = dh + ref[...]
    whole = jnp.concatenate([ref[...].astype(F32) for ref in g_prior] + [g], axis=1)
    grad[...] = (whole + dh).astype(BF16).reshape(groups, bins, chans)
    table = jnp.zeros((hot.shape[0], chans), F32)
    for b in range(groups):
        total = jnp.sum(dh[b * bins : (b + 1) * bins], axis=0, keepdims=True)
        table = table + hot[:, b : b + 1] * (total * scale)
    table_t = table.T.astype(BF16)
    weight_blocks(h_t, taps, scale, keep, send, 3 * width)
    half = chans // 2
    bit = dp_bit(0)
    for ref, part in ((send, 1 - bit), (keep, bit)):
        ref[:, 3 * width :] = jnp.where(part == 0, table_t[0:half], table_t[half:])


def fold_kernel(level, count, *refs):
    summands, out = refs[:count], refs[count:]
    size = out[0].shape[0]
    for offset, ref in enumerate(out):
        part = by_core(*(place_in(bits, mask_of(bits, offset)) for bits in level))
        at = pl.ds(pl.multiple_of(part * size, size), size)
        total = summands[0][at, :].astype(F32)
        for other in summands[1:]:
            total = total + other[at, :].astype(F32)
        ref[...] = total.astype(BF16)


def assemble_kernel(plans, *refs):
    weight_out, table_out, table_t = refs[-3:]
    pieces = list(refs[:-3])
    col = 0
    for width, levels, lists in plans:
        for offsets in lists:
            ref = pieces.pop(0)
            size = ref.shape[0] // len(offsets)
            for slot, (core, masks) in enumerate(offsets):
                blocks = []
                for parity in (0, 1):
                    block = 0
                    for level in levels:
                        bits = level[parity]
                        block = block * (1 << len(bits)) + place_in(bits, masks[parity])
                    blocks.append(block)
                block = by_core(*blocks, other=core == 1)
                half = dp_bit(0) if core == 0 else 1 - dp_bit(0)
                block = block + half * (weight_out.shape[1] // 2 // size)
                row = pl.ds(pl.multiple_of(block * size, size), size)
                here = slice(slot * size, (slot + 1) * size)
                for k in range(3):
                    weight_out[k, row, col : col + width] = ref[here, k * width : (k + 1) * width]
                if ref.shape[1] > 3 * width:
                    table_t[row, :] = ref[here, 3 * width :].astype(F32)
        col += width
    table_out[...] = table_t[...].T[: table_out.shape[0]].astype(BF16)


def swap(value, even, odd=None):
    count = lax.axis_size("dp")
    masks = (even, even if odd is None else odd)
    return lax.ppermute(value, "dp", [(i, i ^ masks[i % 2]) for i in range(count)])


def single(bits):
    return [((a,), (b,)) for a, b in zip(bits, reversed(bits))]


def double(bits):
    pairs = [tuple(bits[n : n + 2]) for n in range(0, len(bits), 2)]
    return [(pair, pair) for pair in pairs]


def offsets_in(level):
    return range(1, 1 << len(level[0]))


def body(section_input, top_grad, conv_weight, step_table, timesteps, dilations):
    section_count = lax.axis_size("section")
    dp_count = lax.axis_size("dp")
    dp_bits = dp_count.bit_length() - 1
    x = section_input[0]
    weight = conv_weight[0]
    table = step_table[0]
    groups, bins, chans = x.shape
    rows = groups * bins
    sent = SENT
    scale = 1.0 / math.sqrt(groups * dp_count * bins)
    unit = 2 * rows * chans * chans * 3
    starts = [sum(sent[:n]) for n in range(len(sent))]

    part = rows // PARTS
    room = pltpu.VMEM((part, 3 * chans), BF16)
    of_part = [
        like((part, chans), F32),
        like((part, 3 * chans), BF16),
        like((part, sent[0]), BF16),
    ]
    far = (timesteps, x, table, weight, top_grad)
    mixed, weight, top, hot, shift, *first = call(
        first_kernel,
        [
            like((rows, chans), BF16),
            like(weight.shape, BF16),
            like(x.shape, BF16),
            like((128, 128), F32),
            like((2 * bins, bins), BF16),
        ]
        + of_part,
        (dilations,) + tuple(pltpu.with_memory_space_constraint(v, pltpu.HBM) for v in far),
        smem=1,
        far=5,
        scratch=[
            pltpu.SMEM(timesteps.shape, jnp.int32),
            pltpu.VMEM(x.shape, BF16),
            pltpu.VMEM(table.shape, BF16),
            pltpu.VMEM(table.shape, F32),
            room,
            pltpu.SemaphoreType.DMA((9,)),
        ],
        flops=2 * unit // PARTS,
    )

    def below(value):
        return lax.ppermute(value, "section", [(i, i - 1) for i in range(1, section_count)])

    made = [first]
    for n in range(1, PARTS):
        made.append(
            call(
                functools.partial(other_kernel, n * part),
                of_part,
                (shift, mixed, weight, top),
                scratch=[room],
                flops=2 * unit // PARTS,
            )
        )
    slope = [v[0] for v in made]
    late = call(
        functools.partial(rest_kernel, sent[0]),
        [like((rows, sent[1]), BF16)],
        (weight, top) + tuple(v[1] for v in made),
        flops=unit // 2,
    )[0]
    got = [[below(v[2]) for v in made], [below(late)]]
    h_t = call(turn_kernel, [like((chans, rows), BF16)], (mixed,), flops=unit // 9)[0]
    for _ in range(section_count - 2):
        pieces = [
            call(
                functools.partial(layer_kernel, n * part),
                [like((part, cols), BF16) for cols in sent],
                (shift, slope[n], weight, top, got[0][n], got[1][0]),
                scratch=[room],
                flops=unit // PARTS,
            )
            for n in range(PARTS)
        ]
        late = jnp.concatenate([v[1] for v in pieces], axis=0)
        got = [[below(v[0]) for v in pieces], [below(late)]]

    inner = list(range(1, dp_bits - 1))
    plans = []
    pieces = []
    before = []
    ahead = None
    used = []
    accs = []
    for n, width in enumerate(sent):
        col = starts[n]
        if ahead is not None and HOLD:
            got[n], _ = lax.optimization_barrier((got[n], ahead))
        recv = tuple(slope) + tuple(got[n])
        if n < len(sent) - 1:
            g_now, taps_now, *blocks = call(
                functools.partial(weight_kernel, col, scale),
                [like((rows, width), BF16), like((rows, 3 * width), BF16)]
                + [like((chans // 2, 3 * width), BF16)] * 2,
                (shift, top, h_t) + recv,
                    flops=unit * width // chans,
            )
            acc = call(
                functools.partial(back_kernel, col),
                [like((rows, chans), F32)],
                (taps_now, weight),
                flops=10**11,
            )[0]
            used.append(g_now)
            accs.append(acc)
        else:
            *blocks, grad = call(
                functools.partial(last_kernel, col, scale, len(used)),
                [like((chans // 2, 3 * width + 128), BF16)] * 2 + [like(x.shape, BF16)],
                (shift, top, h_t, weight, hot) + recv + tuple(used) + tuple(accs),
                    scratch=[pltpu.VMEM((rows, 3 * width), BF16)],
                flops=10**11,
            )
        reduce_by, gather_by = CHAINS[n]
        levels = reduce_by(inner)
        rounds = []

        def ordered(*arrived):
            arrived = list(arrived)
            at = TIES.get(len(rounds))
            rounds.append(arrived)
            if before and at is not None:
                arrived = list(lax.optimization_barrier((*arrived, *before[at]))[: len(arrived)])
            return arrived

        if before and FIRST:
            blocks[1] = lax.optimization_barrier((blocks[1], *before[1]))[0]
        blocks = [blocks[0]] + ordered(swap(blocks[1], 1))
        for level in levels:
            split = 1 << len(level[0])
            blocks = call(
                functools.partial(fold_kernel, level, len(blocks)),
                [like((blocks[0].shape[0] // split, blocks[0].shape[1]), BF16)] * split,
                tuple(blocks),
            )
            ahead = blocks[1]
            arrived = [
                swap(blocks[o], *(mask_of(bits, o) for bits in level)) for o in offsets_in(level)
            ]
            blocks = [blocks[0]] + ordered(*arrived)
        keep = sum(v.astype(F32) for v in blocks).astype(BF16)
        arrived = ordered(swap(keep, 1 << (dp_bits - 1)))
        own = (keep.astype(F32) + arrived[0].astype(F32)).astype(BF16)
        held = [(own, [(0, (0, 0))])]
        for level in reversed(gather_by(inner)):
            message = jnp.concatenate([v for v, _ in held], axis=0) if len(held) > 1 else own
            offsets = [m for _, offs in held for _, m in offs]
            masks = [tuple(mask_of(bits, o) for bits in level) for o in offsets_in(level)]
            arrived = ordered(*(swap(message, *mask) for mask in masks))
            held += [
                (v, [(0, (m[0] ^ e, m[1] ^ o)) for m in offsets]) for v, (e, o) in zip(arrived, masks)
            ]
        message = jnp.concatenate([v for v, _ in held], axis=0)
        masks = [m for _, offs in held for _, m in offs]
        held.append((ordered(swap(message, 1))[0], [(1, m) for m in masks]))
        pieces += [v for v, _ in held]
        plans.append((width, levels, [offs for _, offs in held]))
        before = rounds

    weight_out, table_out = call(
        functools.partial(assemble_kernel, plans),
        [like(weight.shape, BF16), like(table.shape, BF16)],
        tuple(pieces),
        scratch=[pltpu.VMEM((chans, 128), F32)],
    )
    return (grad[None], weight_out[None], table_out[None])


CHAINS = ((single, single), (single, double))
TIES = {4: 5}
FIRST = True
HOLD = False


def solution(mesh):
    placed = (
        P("section", "dp", None, None),
        P("dp", None, None),
        P("section", None, None, None),
        P("section", None, None),
        P("dp"),
        P("section"),
    )
    return jax.shard_map(
        body,
        mesh=mesh,
        in_specs=placed,
        out_specs=(
            P("section", "dp", None, None),
            P("section", None, None, None),
            P("section", None, None),
        ),
        check_vma=False,
    )
```

```python
import functools
import math

import jax
import jax.numpy as jnp
from jax import lax
from jax.experimental import pallas as pl
from jax.experimental.pallas import tpu as pltpu
from jax.sharding import PartitionSpec as P

SENT = (256, 256)
PARTS = 2
F32 = jnp.float32
BF16 = jnp.bfloat16
VMEM = pl.BlockSpec(memory_space=pltpu.VMEM)
SMEM = pl.BlockSpec(memory_space=pltpu.SMEM)
HBM = pl.BlockSpec(memory_space=pltpu.HBM)
NT = (((1,), (1,)), ((), ()))


def call(kernel, out_shape, args, smem=0, far=0, scratch=(), flops=0):
    specs = [SMEM] * smem + [HBM] * far + [VMEM] * (len(args) - smem - far)
    moved = sum(a.size * a.dtype.itemsize for a in args)
    moved += sum(math.prod(o.shape) * o.dtype.itemsize for o in out_shape)
    return pl.pallas_call(
        kernel,
        out_shape=out_shape,
        in_specs=specs,
        out_specs=[VMEM] * len(out_shape),
        scratch_shapes=list(scratch),
        compiler_params=pltpu.CompilerParams(vmem_limit_bytes=32 * 2**20),
        cost_estimate=pl.CostEstimate(flops=flops, bytes_accessed=moved, transcendentals=0),
    )(*args)


def is_top():
    return lax.axis_index("section") == lax.axis_size("section") - 1


def dp_bit(n):
    return lax.rem(lax.div(lax.axis_index("dp"), 1 << n), 2)


def like(shape, dtype):
    return jax.ShapeDtypeStruct(shape, dtype)


def shift_matrix(bins, dilation):
    row = lax.broadcasted_iota(jnp.int32, (bins, bins), 0)
    col = lax.broadcasted_iota(jnp.int32, (bins, bins), 1)
    both = [jnp.where(col == row + by, 1.0, 0.0).astype(BF16) for by in (-dilation, dilation)]
    return jnp.concatenate(both, axis=0)


def put_taps(values, taps, shift, orientation):
    rows, cols = values.shape
    bins = shift.shape[1]
    taps[:, cols : 2 * cols] = values
    for b in range(rows // bins):
        at = slice(b * bins, (b + 1) * bins)
        moved = jnp.dot(shift[...], values[at], preferred_element_type=F32).astype(BF16)
        earlier, later = moved[:bins], moved[bins:]
        first, third = (earlier, later) if orientation == 1 else (later, earlier)
        taps[at, 0:cols] = first
        taps[at, 2 * cols : 3 * cols] = third


def back_product(taps, weight, cols):
    total = None
    for k in range(3):
        part = lax.dot_general(
            taps[:, k * cols : (k + 1) * cols], weight[k], NT, preferred_element_type=F32
        )
        total = part if total is None else total + part
    return total


def forward(h, taps, shift, weight, slope, wait=None):
    put_taps(h, taps, shift, 1)
    chans = h.shape[1]
    y = None
    for k in range(3):
        if wait is not None:
            wait(k)
        part = jnp.dot(taps[:, k * chans : (k + 1) * chans], weight[k], preferred_element_type=F32)
        y = part if y is None else y + part
    gate = jax.nn.sigmoid(y)
    slope[...] = gate * (1.0 + y * (1.0 - gate))


def backward(g, taps, shift, slope):
    delta = (g * slope[...]).astype(BF16)
    put_taps(delta, taps, shift, -1)


def below_of(g, taps, weight, col, out):
    cols = slice(col, col + out.shape[1])
    dh = back_product(taps, weight[:, cols, :], weight.shape[2])
    out[...] = (g[:, cols].astype(F32) + dh).astype(BF16)


def first_kernel(dil, ts, x, table, weight, top, mixed, weight_v, top_v, hot, shift, *rest):
    slope, taps, g_out, ts_s, x_v, table_v, tab, forward_taps, sems = rest
    groups, bins, chans = x.shape
    rows = slope.shape[0]
    near = slice(0, rows // bins)
    others = slice(rows // bins, groups)
    pairs = [(ts, ts_s), (table, table_v), (x.at[near], x_v.at[near])]
    pairs += [(weight.at[k], weight_v.at[k]) for k in range(3)]
    pairs += [(top.at[near], top_v.at[near]), (x.at[others], x_v.at[others]), (top.at[others], top_v.at[others])]
    copies = [pltpu.make_async_copy(a, b, sems.at[n]) for n, (a, b) in enumerate(pairs)]
    for copy in copies:
        copy.start()
    shift[...] = shift_matrix(bins, dil[0])
    for copy in copies[:3]:
        copy.wait()
    tab[...] = table_v[...].astype(F32)

    def mix(b):
        row = x_v[b].astype(F32) + tab[pl.ds(ts_s[b], 1), :]
        mixed[b * bins : (b + 1) * bins, :] = row.astype(BF16)

    for b in range(rows // bins):
        mix(b)
    forward(
        mixed[0:rows, :], forward_taps, shift, weight_v, slope, lambda k: copies[3 + k].wait()
    )
    copies[6].wait()
    g = top_v[near].reshape(rows, chans)
    backward(g.astype(F32), taps, shift, slope)
    below_of(g, taps, weight_v, 0, g_out)
    steps = lax.broadcasted_iota(jnp.int32, hot.shape, 0)
    lanes = lax.broadcasted_iota(jnp.int32, hot.shape, 1)
    marks = jnp.zeros(hot.shape, F32)
    for b in range(groups):
        marks = jnp.where((lanes == b) & (steps == ts_s[b]), 1.0, marks)
    hot[...] = marks
    copies[7].wait()
    for b in range(rows // bins, groups):
        mix(b)
    copies[8].wait()


def other_kernel(start, shift, mixed, weight, top, slope, taps, g_out, forward_taps):
    at = slice(start, start + slope.shape[0])
    forward(mixed[at, :], forward_taps, shift, weight, slope)
    g = top[...].reshape(mixed.shape)[at]
    backward(g.astype(F32), taps, shift, slope)
    below_of(g, taps, weight, 0, g_out)


def rest_kernel(col, weight, top, *rest):
    taps, g_out = rest[:-1], rest[-1]
    part = taps[0].shape[0]
    g = top[...].reshape(-1, top.shape[2])
    for n, ref in enumerate(taps):
        at = slice(n * part, (n + 1) * part)
        below_of(g[at], ref, weight, col, g_out.at[at])


def turn_kernel(mixed, h_t):
    h_t[...] = mixed[...].T


def layer_kernel(start, shift, slope, weight, top, *rest):
    early, late, out, out_late, taps = rest
    rows = slope.shape[0]
    got = jnp.concatenate([early[...], late[start : start + rows]], axis=1)
    fresh = top[...].reshape(-1, top.shape[2])[start : start + rows]
    g = jnp.where(is_top(), fresh.astype(F32), got.astype(F32))
    backward(g, taps, shift, slope)
    below_of(g, taps, weight, 0, out)
    below_of(g, taps, weight, out.shape[1], out_late)


def upstream(col, top, recv):
    got = [ref[...].astype(F32) for ref in recv]
    got = got[0] if len(got) == 1 else jnp.concatenate(got, axis=0)
    rows, width = got.shape
    fresh = top[...].reshape(rows, top.shape[-1])[:, col : col + width]
    return jnp.where(is_top(), fresh.astype(F32), got)


def delta_of(g, slope, col):
    width = g.shape[1]
    factor = jnp.concatenate([ref[:, col : col + width] for ref in slope], axis=0)
    return (g * factor).astype(BF16)


def by_core(even, odd, other=False):
    return jnp.where(dp_bit(0) == (1 if other else 0), even, odd)


def place_in(bits, mask=0):
    place = 0
    for n in reversed(bits):
        place = place * 2 + (1 - dp_bit(n) if (mask >> n) & 1 else dp_bit(n))
    return place


def mask_of(bits, offset):
    return sum(1 << n for j, n in enumerate(bits) if (offset >> j) & 1)


def weight_blocks(h_t, taps, scale, keep, send, cols):
    half = h_t.shape[0] // 2
    bit = dp_bit(0)
    for ref, part in ((keep, bit), (send, 1 - bit)):
        left = h_t[pl.ds(pl.multiple_of(part * half, half), half), :]
        prod = jnp.dot(left, taps[...], preferred_element_type=F32)
        ref[:, 0:cols] = (prod * scale).astype(BF16)


def weight_kernel(col, scale, shift, top, h_t, *rest):
    slope, recv, out = rest[:PARTS], rest[PARTS:-4], rest[-4:]
    g_used, taps, keep, send = out
    width = g_used.shape[1]
    g = upstream(col, top, recv)
    g_used[...] = g.astype(BF16)
    delta = delta_of(g, slope, col)
    put_taps(delta, taps, shift, -1)
    weight_blocks(h_t, taps, scale, keep, send, 3 * width)


def back_kernel(col, taps, weight, acc):
    width = taps.shape[1] // 3
    acc[...] = back_product(taps, weight[:, :, col : col + width], width)


def last_kernel(col, scale, prior, shift, top, h_t, weight, hot, *rest):
    slope, recv = rest[:PARTS], rest[PARTS : -4 - 2 * prior]
    g_prior, acc = rest[-4 - 2 * prior : -4 - prior], rest[-4 - prior : -4]
    keep, send, grad, taps = rest[-4:]
    groups, bins, chans = grad.shape
    width = taps.shape[1] // 3
    g = upstream(col, top, recv)
    delta = delta_of(g, slope, col)
    put_taps(delta, taps, shift, -1)
    dh = back_product(taps, weight[:, :, col : col + width], width)
    for ref in acc:
        dh = dh + ref[...]
    whole = jnp.concatenate([ref[...].astype(F32) for ref in g_prior] + [g], axis=1)
    grad[...] = (whole + dh).astype(BF16).reshape(groups, bins, chans)
    table = jnp.zeros((hot.shape[0], chans), F32)
    for b in range(groups):
        total = jnp.sum(dh[b * bins : (b + 1) * bins], axis=0, keepdims=True)
        table = table + hot[:, b : b + 1] * (total * scale)
    table_t = table.T.astype(BF16)
    weight_blocks(h_t, taps, scale, keep, send, 3 * width)
    half = chans // 2
    bit = dp_bit(0)
    for ref, part in ((send, 1 - bit), (keep, bit)):
        ref[:, 3 * width :] = jnp.where(part == 0, table_t[0:half], table_t[half:])


def fold_kernel(level, count, *refs):
    summands, out = refs[:count], refs[count:]
    size = out[0].shape[0]
    for offset, ref in enumerate(out):
        part = by_core(*(place_in(bits, mask_of(bits, offset)) for bits in level))
        at = pl.ds(pl.multiple_of(part * size, size), size)
        total = summands[0][at, :].astype(F32)
        for other in summands[1:]:
            total = total + other[at, :].astype(F32)
        ref[...] = total.astype(BF16)


def assemble_kernel(plans, *refs):
    weight_out, table_out, table_t = refs[-3:]
    pieces = list(refs[:-3])
    col = 0
    for width, total, levels, lists in plans:
        for left, offsets in lists:
            ref = pieces.pop(0)
            size = ref.shape[0] // len(offsets)
            for slot, (core, masks) in enumerate(offsets):
                blocks = []
                for parity in (0, 1):
                    block = 0
                    for level in levels:
                        bits = level[parity]
                        block = block * (1 << len(bits)) + place_in(bits, masks[parity])
                    blocks.append(block)
                block = by_core(*blocks, other=core == 1)
                half = dp_bit(0) if core == 0 else 1 - dp_bit(0)
                block = block + half * (weight_out.shape[1] // 2 // size)
                row = pl.ds(pl.multiple_of(block * size, size), size)
                here = slice(slot * size, (slot + 1) * size)
                for k in range(3):
                    weight_out[k, row, col : col + width] = ref[
                        here, left + k * width : left + (k + 1) * width
                    ]
                if total > 3 * width:
                    table_t[row, :] = ref[here, left + 3 * width : left + total].astype(F32)
        col += width
    table_out[...] = table_t[...].T[: table_out.shape[0]].astype(BF16)


def swap(value, even, odd=None):
    count = lax.axis_size("dp")
    masks = (even, even if odd is None else odd)
    return lax.ppermute(value, "dp", [(i, i ^ masks[i % 2]) for i in range(count)])


def single(bits):
    return [((a,), (b,)) for a, b in zip(bits, reversed(bits))]


def double(bits):
    pairs = [tuple(bits[n : n + 2]) for n in range(0, len(bits), 2)]
    return [(pair, pair) for pair in pairs]


def offsets_in(level):
    return range(1, 1 << len(level[0]))


def body(section_input, top_grad, conv_weight, step_table, timesteps, dilations):
    section_count = lax.axis_size("section")
    dp_count = lax.axis_size("dp")
    dp_bits = dp_count.bit_length() - 1
    x = section_input[0]
    weight = conv_weight[0]
    table = step_table[0]
    groups, bins, chans = x.shape
    rows = groups * bins
    sent = SENT
    scale = 1.0 / math.sqrt(groups * dp_count * bins)
    unit = 2 * rows * chans * chans * 3
    starts = [sum(sent[:n]) for n in range(len(sent))]

    part = rows // PARTS
    room = pltpu.VMEM((part, 3 * chans), BF16)
    of_part = [
        like((part, chans), F32),
        like((part, 3 * chans), BF16),
        like((part, sent[0]), BF16),
    ]
    far = (timesteps, x, table, weight, top_grad)
    mixed, weight, top, hot, shift, *first = call(
        first_kernel,
        [
            like((rows, chans), BF16),
            like(weight.shape, BF16),
            like(x.shape, BF16),
            like((128, 128), F32),
            like((2 * bins, bins), BF16),
        ]
        + of_part,
        (dilations,) + tuple(pltpu.with_memory_space_constraint(v, pltpu.HBM) for v in far),
        smem=1,
        far=5,
        scratch=[
            pltpu.SMEM(timesteps.shape, jnp.int32),
            pltpu.VMEM(x.shape, BF16),
            pltpu.VMEM(table.shape, BF16),
            pltpu.VMEM(table.shape, F32),
            room,
            pltpu.SemaphoreType.DMA((9,)),
        ],
        flops=2 * unit // PARTS,
    )

    def below(value):
        pairs = [(i, i - 1) for i in range(1, section_count)]
        if section_count == 2:
            pairs.append((0, 1))
        return lax.ppermute(value, "section", pairs)

    made = [first]
    for n in range(1, PARTS):
        made.append(
            call(
                functools.partial(other_kernel, n * part),
                of_part,
                (shift, mixed, weight, top),
                scratch=[room],
                flops=2 * unit // PARTS,
            )
        )
    slope = [v[0] for v in made]
    late = call(
        functools.partial(rest_kernel, sent[0]),
        [like((rows, sent[1]), BF16)],
        (weight, top) + tuple(v[1] for v in made),
        flops=unit // 2,
    )[0]
    got = [[below(v[2]) for v in made], [below(late)]]
    h_t = call(turn_kernel, [like((chans, rows), BF16)], (mixed,), flops=unit // 9)[0]
    for _ in range(section_count - 2):
        pieces = [
            call(
                functools.partial(layer_kernel, n * part),
                [like((part, cols), BF16) for cols in sent],
                (shift, slope[n], weight, top, got[0][n], got[1][0]),
                scratch=[room],
                flops=unit // PARTS,
            )
            for n in range(PARTS)
        ]
        late = jnp.concatenate([v[1] for v in pieces], axis=0)
        got = [[below(v[0]) for v in pieces], [below(late)]]

    inner = list(range(1, dp_bits - 1))
    gathered = []
    before = []
    ahead = None
    used = []
    accs = []
    for n, width in enumerate(sent):
        col = starts[n]
        if ahead is not None and HOLD:
            got[n], _ = lax.optimization_barrier((got[n], ahead))
        recv = tuple(slope) + tuple(got[n])
        if n < len(sent) - 1:
            g_now, taps_now, *blocks = call(
                functools.partial(weight_kernel, col, scale),
                [like((rows, width), BF16), like((rows, 3 * width), BF16)]
                + [like((chans // 2, 3 * width), BF16)] * 2,
                (shift, top, h_t) + recv,
                    flops=unit * width // chans,
            )
            acc = call(
                functools.partial(back_kernel, col),
                [like((rows, chans), F32)],
                (taps_now, weight),
                flops=10**11,
            )[0]
            used.append(g_now)
            accs.append(acc)
        else:
            *blocks, grad = call(
                functools.partial(last_kernel, col, scale, len(used)),
                [like((chans // 2, 3 * width + 128), BF16)] * 2 + [like(x.shape, BF16)],
                (shift, top, h_t, weight, hot) + recv + tuple(used) + tuple(accs),
                    scratch=[pltpu.VMEM((rows, 3 * width), BF16)],
                flops=10**11,
            )
        reduce_by, gather_by = CHAINS[n]
        levels = reduce_by(inner)
        rounds = []

        def ordered(*arrived):
            arrived = list(arrived)
            at = TIES.get(len(rounds))
            rounds.append(arrived)
            if before and at is not None:
                arrived = list(lax.optimization_barrier((*arrived, *before[at]))[: len(arrived)])
            return arrived

        if before and FIRST:
            blocks[1] = lax.optimization_barrier((blocks[1], *before[1]))[0]
        blocks = [blocks[0]] + ordered(swap(blocks[1], 1))
        for level in levels:
            split = 1 << len(level[0])
            blocks = call(
                functools.partial(fold_kernel, level, len(blocks)),
                [like((blocks[0].shape[0] // split, blocks[0].shape[1]), BF16)] * split,
                tuple(blocks),
            )
            ahead = blocks[1]
            arrived = [
                swap(blocks[o], *(mask_of(bits, o) for bits in level)) for o in offsets_in(level)
            ]
            blocks = [blocks[0]] + ordered(*arrived)
        keep = sum(v.astype(F32) for v in blocks).astype(BF16)
        arrived = ordered(swap(keep, 1 << (dp_bits - 1)))
        own = (keep.astype(F32) + arrived[0].astype(F32)).astype(BF16)
        held = [(own, [(0, (0, 0))])]
        for level in reversed(gather_by(inner)):
            message = jnp.concatenate([v for v, _ in held], axis=0) if len(held) > 1 else own
            offsets = [m for _, offs in held for _, m in offs]
            masks = [tuple(mask_of(bits, o) for bits in level) for o in offsets_in(level)]
            arrived = ordered(*(swap(message, *mask) for mask in masks))
            held += [
                (v, [(0, (m[0] ^ e, m[1] ^ o)) for m in offsets]) for v, (e, o) in zip(arrived, masks)
            ]
        gathered.append((width, levels, held))
        before = rounds

    both = [jnp.concatenate([v for v, _ in held], axis=0) for _, _, held in gathered]
    crossed = swap(jnp.concatenate(both, axis=1), 1)
    plans = []
    pieces = []
    at = 0
    for width, levels, held in gathered:
        lists = [(0, offs) for _, offs in held] + [(at, [(1, m) for _, offs in held for _, m in offs])]
        plans.append((width, held[0][0].shape[1], levels, lists))
        pieces += [v for v, _ in held] + [crossed]
        at += held[0][0].shape[1]

    weight_out, table_out = call(
        functools.partial(assemble_kernel, plans),
        [like(weight.shape, BF16), like(table.shape, BF16)],
        tuple(pieces),
        scratch=[pltpu.VMEM((chans, 128), F32)],
    )
    return (grad[None], weight_out[None], table_out[None])


CHAINS = ((single, single), (single, double))
TIES = {4: 5}
FIRST = True
HOLD = False


def solution(mesh):
    placed = (
        P("section", "dp", None, None),
        P("dp", None, None),
        P("section", None, None, None),
        P("section", None, None),
        P("dp"),
        P("section"),
    )
    return jax.shard_map(
        body,
        mesh=mesh,
        in_specs=placed,
        out_specs=(
            P("section", "dp", None, None),
            P("section", None, None, None),
            P("section", None, None),
        ),
        check_vma=False,
    )
```

```python
import functools
import math

import jax
import jax.numpy as jnp
from jax import lax
from jax.experimental import pallas as pl
from jax.experimental.pallas import tpu as pltpu
from jax.sharding import PartitionSpec as P

SENT = (256, 256)
PARTS = 2
F32 = jnp.float32
BF16 = jnp.bfloat16
VMEM = pl.BlockSpec(memory_space=pltpu.VMEM)
SMEM = pl.BlockSpec(memory_space=pltpu.SMEM)
HBM = pl.BlockSpec(memory_space=pltpu.HBM)
NT = (((1,), (1,)), ((), ()))


def call(kernel, out_shape, args, smem=0, far=0, scratch=(), flops=0):
    specs = [SMEM] * smem + [HBM] * far + [VMEM] * (len(args) - smem - far)
    moved = sum(a.size * a.dtype.itemsize for a in args)
    moved += sum(math.prod(o.shape) * o.dtype.itemsize for o in out_shape)
    return pl.pallas_call(
        kernel,
        out_shape=out_shape,
        in_specs=specs,
        out_specs=[VMEM] * len(out_shape),
        scratch_shapes=list(scratch),
        compiler_params=pltpu.CompilerParams(vmem_limit_bytes=32 * 2**20),
        cost_estimate=pl.CostEstimate(flops=flops, bytes_accessed=moved, transcendentals=0),
    )(*args)


def is_top():
    return lax.axis_index("section") == lax.axis_size("section") - 1


def dp_bit(n):
    return lax.rem(lax.div(lax.axis_index("dp"), 1 << n), 2)


def like(shape, dtype):
    return jax.ShapeDtypeStruct(shape, dtype)


def shift_matrix(bins, dilation):
    row = lax.broadcasted_iota(jnp.int32, (bins, bins), 0)
    col = lax.broadcasted_iota(jnp.int32, (bins, bins), 1)
    both = [jnp.where(col == row + by, 1.0, 0.0).astype(BF16) for by in (-dilation, dilation)]
    return jnp.concatenate(both, axis=0)


def put_taps(values, taps, shift, orientation):
    rows, cols = values.shape
    bins = shift.shape[1]
    taps[:, cols : 2 * cols] = values
    for b in range(rows // bins):
        at = slice(b * bins, (b + 1) * bins)
        moved = jnp.dot(shift[...], values[at], preferred_element_type=F32).astype(BF16)
        earlier, later = moved[:bins], moved[bins:]
        first, third = (earlier, later) if orientation == 1 else (later, earlier)
        taps[at, 0:cols] = first
        taps[at, 2 * cols : 3 * cols] = third


def back_product(taps, weight, cols):
    total = None
    for k in range(3):
        part = lax.dot_general(
            taps[:, k * cols : (k + 1) * cols], weight[k], NT, preferred_element_type=F32
        )
        total = part if total is None else total + part
    return total


def forward(h, taps, shift, weight, slope, wait=None):
    put_taps(h, taps, shift, 1)
    chans = h.shape[1]
    y = None
    for k in range(3):
        if wait is not None:
            wait(k)
        part = jnp.dot(taps[:, k * chans : (k + 1) * chans], weight[k], preferred_element_type=F32)
        y = part if y is None else y + part
    gate = jax.nn.sigmoid(y)
    slope[...] = gate * (1.0 + y * (1.0 - gate))


def backward(g, taps, shift, slope):
    delta = (g * slope[...]).astype(BF16)
    put_taps(delta, taps, shift, -1)


def below_of(g, taps, weight, col, out):
    cols = slice(col, col + out.shape[1])
    dh = back_product(taps, weight[:, cols, :], weight.shape[2])
    out[...] = (g[:, cols].astype(F32) + dh).astype(BF16)


def first_kernel(dil, ts, x, table, weight, top, mixed, weight_v, top_v, hot, shift, *rest):
    slope, taps, g_out, ts_s, x_v, table_v, tab, forward_taps, sems = rest
    groups, bins, chans = x.shape
    rows = slope.shape[0]
    near = slice(0, rows // bins)
    others = slice(rows // bins, groups)
    pairs = [(ts, ts_s), (table, table_v), (x.at[near], x_v.at[near])]
    pairs += [(weight.at[k], weight_v.at[k]) for k in range(3)]
    pairs += [(top.at[near], top_v.at[near]), (x.at[others], x_v.at[others]), (top.at[others], top_v.at[others])]
    copies = [pltpu.make_async_copy(a, b, sems.at[n]) for n, (a, b) in enumerate(pairs)]
    for copy in copies:
        copy.start()
    shift[...] = shift_matrix(bins, dil[0])
    for copy in copies[:3]:
        copy.wait()
    tab[...] = table_v[...].astype(F32)

    def mix(b):
        row = x_v[b].astype(F32) + tab[pl.ds(ts_s[b], 1), :]
        mixed[b * bins : (b + 1) * bins, :] = row.astype(BF16)

    for b in range(rows // bins):
        mix(b)

    @pl.when(is_top())
    def _():
        def arrived(k):
            copies[3 + k].wait()

        forward(mixed[0:rows, :], forward_taps, shift, weight_v, slope, arrived)
        copies[6].wait()
        g = top_v[near].reshape(rows, chans)
        backward(g.astype(F32), taps, shift, slope)
        below_of(g, taps, weight_v, 0, g_out)

    @pl.when(jnp.logical_not(is_top()))
    def _():
        for copy in copies[3:7]:
            copy.wait()
        g_out[...] = jnp.zeros(g_out.shape, BF16)

    steps = lax.broadcasted_iota(jnp.int32, hot.shape, 0)
    lanes = lax.broadcasted_iota(jnp.int32, hot.shape, 1)
    marks = jnp.zeros(hot.shape, F32)
    for b in range(groups):
        marks = jnp.where((lanes == b) & (steps == ts_s[b]), 1.0, marks)
    hot[...] = marks
    copies[7].wait()
    for b in range(rows // bins, groups):
        mix(b)
    copies[8].wait()


def other_kernel(start, shift, mixed, weight, top, slope, taps, g_out, forward_taps):
    @pl.when(is_top())
    def _():
        at = slice(start, start + slope.shape[0])
        forward(mixed[at, :], forward_taps, shift, weight, slope)
        g = top[...].reshape(mixed.shape)[at]
        backward(g.astype(F32), taps, shift, slope)
        below_of(g, taps, weight, 0, g_out)

    @pl.when(jnp.logical_not(is_top()))
    def _():
        g_out[...] = jnp.zeros(g_out.shape, BF16)


def rest_kernel(col, weight, top, *rest):
    taps, g_out = rest[:-1], rest[-1]
    part = taps[0].shape[0]

    @pl.when(is_top())
    def _():
        g = top[...].reshape(-1, top.shape[2])
        for n, ref in enumerate(taps):
            at = slice(n * part, (n + 1) * part)
            below_of(g[at], ref, weight, col, g_out.at[at])

    @pl.when(jnp.logical_not(is_top()))
    def _():
        g_out[...] = jnp.zeros(g_out.shape, BF16)


def prepare_kernel(shift, mixed, weight, *rest):
    early, h_t, late, taps = rest[:PARTS], rest[PARTS], rest[PARTS + 1 : -1], rest[-1]
    part = taps.shape[0]
    h_t[...] = mixed[...].T

    @pl.when(is_top())
    def _():
        for n in range(PARTS):
            late[n][...] = early[n][...]

    @pl.when(jnp.logical_not(is_top()))
    def _():
        for n in range(PARTS):
            forward(mixed[n * part : (n + 1) * part, :], taps, shift, weight, late[n])


def layer_kernel(start, shift, slope, weight, top, *rest):
    early, late, out, out_late, taps = rest
    rows = slope.shape[0]
    got = jnp.concatenate([early[...], late[start : start + rows]], axis=1)
    fresh = top[...].reshape(-1, top.shape[2])[start : start + rows]
    g = jnp.where(is_top(), fresh.astype(F32), got.astype(F32))
    backward(g, taps, shift, slope)
    below_of(g, taps, weight, 0, out)
    below_of(g, taps, weight, out.shape[1], out_late)


def upstream(col, top, recv):
    got = [ref[...].astype(F32) for ref in recv]
    got = got[0] if len(got) == 1 else jnp.concatenate(got, axis=0)
    rows, width = got.shape
    fresh = top[...].reshape(rows, top.shape[-1])[:, col : col + width]
    return jnp.where(is_top(), fresh.astype(F32), got)


def delta_of(g, slope, col):
    width = g.shape[1]
    factor = jnp.concatenate([ref[:, col : col + width] for ref in slope], axis=0)
    return (g * factor).astype(BF16)


def by_core(even, odd, other=False):
    return jnp.where(dp_bit(0) == (1 if other else 0), even, odd)


def place_in(bits, mask=0):
    place = 0
    for n in reversed(bits):
        place = place * 2 + (1 - dp_bit(n) if (mask >> n) & 1 else dp_bit(n))
    return place


def mask_of(bits, offset):
    return sum(1 << n for j, n in enumerate(bits) if (offset >> j) & 1)


def weight_blocks(h_t, taps, scale, keep, send, cols):
    half = h_t.shape[0] // 2
    bit = dp_bit(0)
    for ref, part in ((keep, bit), (send, 1 - bit)):
        left = h_t[pl.ds(pl.multiple_of(part * half, half), half), :]
        prod = jnp.dot(left, taps[...], preferred_element_type=F32)
        ref[:, 0:cols] = (prod * scale).astype(BF16)


def weight_kernel(col, scale, shift, top, h_t, *rest):
    slope, recv, out = rest[:PARTS], rest[PARTS:-4], rest[-4:]
    g_used, taps, keep, send = out
    width = g_used.shape[1]
    g = upstream(col, top, recv)
    g_used[...] = g.astype(BF16)
    delta = delta_of(g, slope, col)
    put_taps(delta, taps, shift, -1)
    weight_blocks(h_t, taps, scale, keep, send, 3 * width)


def back_kernel(col, taps, weight, acc):
    width = taps.shape[1] // 3
    acc[...] = back_product(taps, weight[:, :, col : col + width], width)


def last_kernel(col, scale, prior, shift, top, h_t, weight, hot, *rest):
    slope, recv = rest[:PARTS], rest[PARTS : -4 - 2 * prior]
    g_prior, acc = rest[-4 - 2 * prior : -4 - prior], rest[-4 - prior : -4]
    keep, send, grad, taps = rest[-4:]
    groups, bins, chans = grad.shape
    width = taps.shape[1] // 3
    g = upstream(col, top, recv)
    delta = delta_of(g, slope, col)
    put_taps(delta, taps, shift, -1)
    dh = back_product(taps, weight[:, :, col : col + width], width)
    for ref in acc:
        dh = dh + ref[...]
    whole = jnp.concatenate([ref[...].astype(F32) for ref in g_prior] + [g], axis=1)
    grad[...] = (whole + dh).astype(BF16).reshape(groups, bins, chans)
    table = jnp.zeros((hot.shape[0], chans), F32)
    for b in range(groups):
        total = jnp.sum(dh[b * bins : (b + 1) * bins], axis=0, keepdims=True)
        table = table + hot[:, b : b + 1] * (total * scale)
    table_t = table.T.astype(BF16)
    weight_blocks(h_t, taps, scale, keep, send, 3 * width)
    half = chans // 2
    bit = dp_bit(0)
    for ref, part in ((send, 1 - bit), (keep, bit)):
        ref[:, 3 * width :] = jnp.where(part == 0, table_t[0:half], table_t[half:])


def fold_kernel(level, count, *refs):
    summands, out = refs[:count], refs[count:]
    size = out[0].shape[0]
    for offset, ref in enumerate(out):
        part = by_core(*(place_in(bits, mask_of(bits, offset)) for bits in level))
        at = pl.ds(pl.multiple_of(part * size, size), size)
        total = summands[0][at, :].astype(F32)
        for other in summands[1:]:
            total = total + other[at, :].astype(F32)
        ref[...] = total.astype(BF16)


def assemble_kernel(plans, *refs):
    weight_out, table_out, table_t = refs[-3:]
    pieces = list(refs[:-3])
    col = 0
    for width, total, levels, lists in plans:
        for left, offsets in lists:
            ref = pieces.pop(0)
            size = ref.shape[0] // len(offsets)
            for slot, (core, masks) in enumerate(offsets):
                blocks = []
                for parity in (0, 1):
                    block = 0
                    for level in levels:
                        bits = level[parity]
                        block = block * (1 << len(bits)) + place_in(bits, masks[parity])
                    blocks.append(block)
                block = by_core(*blocks, other=core == 1)
                half = dp_bit(0) if core == 0 else 1 - dp_bit(0)
                block = block + half * (weight_out.shape[1] // 2 // size)
                row = pl.ds(pl.multiple_of(block * size, size), size)
                here = slice(slot * size, (slot + 1) * size)
                for k in range(3):
                    weight_out[k, row, col : col + width] = ref[
                        here, left + k * width : left + (k + 1) * width
                    ]
                if total > 3 * width:
                    table_t[row, :] = ref[here, left + 3 * width : left + total].astype(F32)
        col += width
    table_out[...] = table_t[...].T[: table_out.shape[0]].astype(BF16)


def swap(value, even, odd=None):
    count = lax.axis_size("dp")
    masks = (even, even if odd is None else odd)
    return lax.ppermute(value, "dp", [(i, i ^ masks[i % 2]) for i in range(count)])


def single(bits):
    return [((a,), (b,)) for a, b in zip(bits, reversed(bits))]


def double(bits):
    pairs = [tuple(bits[n : n + 2]) for n in range(0, len(bits), 2)]
    return [(pair, pair) for pair in pairs]


def offsets_in(level):
    return range(1, 1 << len(level[0]))


def body(section_input, top_grad, conv_weight, step_table, timesteps, dilations):
    section_count = lax.axis_size("section")
    dp_count = lax.axis_size("dp")
    dp_bits = dp_count.bit_length() - 1
    x = section_input[0]
    weight = conv_weight[0]
    table = step_table[0]
    groups, bins, chans = x.shape
    rows = groups * bins
    sent = SENT
    scale = 1.0 / math.sqrt(groups * dp_count * bins)
    unit = 2 * rows * chans * chans * 3
    starts = [sum(sent[:n]) for n in range(len(sent))]

    part = rows // PARTS
    room = pltpu.VMEM((part, 3 * chans), BF16)
    of_part = [
        like((part, chans), F32),
        like((part, 3 * chans), BF16),
        like((part, sent[0]), BF16),
    ]
    far = (timesteps, x, table, weight, top_grad)
    mixed, weight, top, hot, shift, *first = call(
        first_kernel,
        [
            like((rows, chans), BF16),
            like(weight.shape, BF16),
            like(x.shape, BF16),
            like((128, 128), F32),
            like((2 * bins, bins), BF16),
        ]
        + of_part,
        (dilations,) + tuple(pltpu.with_memory_space_constraint(v, pltpu.HBM) for v in far),
        smem=1,
        far=5,
        scratch=[
            pltpu.SMEM(timesteps.shape, jnp.int32),
            pltpu.VMEM(x.shape, BF16),
            pltpu.VMEM(table.shape, BF16),
            pltpu.VMEM(table.shape, F32),
            room,
            pltpu.SemaphoreType.DMA((9,)),
        ],
        flops=2 * unit // PARTS,
    )

    def below(value):
        pairs = [(i, i - 1) for i in range(1, section_count)]
        if section_count == 2:
            pairs.append((0, 1))
        return lax.ppermute(value, "section", pairs)

    made = [first]
    for n in range(1, PARTS):
        made.append(
            call(
                functools.partial(other_kernel, n * part),
                of_part,
                (shift, mixed, weight, top),
                scratch=[room],
                flops=2 * unit // PARTS,
            )
        )
    slope = [v[0] for v in made]
    late = call(
        functools.partial(rest_kernel, sent[0]),
        [like((rows, sent[1]), BF16)],
        (weight, top) + tuple(v[1] for v in made),
        flops=unit // 2,
    )[0]
    got = [[below(v[2]) for v in made], [below(late)]]
    h_t, *slope = call(
        prepare_kernel,
        [like((chans, rows), BF16)] + [like((part, chans), F32)] * PARTS,
        (shift, mixed, weight) + tuple(slope),
        scratch=[room],
        flops=unit // 9,
    )
    for _ in range(section_count - 2):
        pieces = [
            call(
                functools.partial(layer_kernel, n * part),
                [like((part, cols), BF16) for cols in sent],
                (shift, slope[n], weight, top, got[0][n], got[1][0]),
                scratch=[room],
                flops=unit // PARTS,
            )
            for n in range(PARTS)
        ]
        late = jnp.concatenate([v[1] for v in pieces], axis=0)
        got = [[below(v[0]) for v in pieces], [below(late)]]

    inner = list(range(1, dp_bits - 1))
    gathered = []
    before = []
    ahead = None
    used = []
    accs = []
    for n, width in enumerate(sent):
        col = starts[n]
        if ahead is not None and HOLD:
            got[n], _ = lax.optimization_barrier((got[n], ahead))
        recv = tuple(slope) + tuple(got[n])
        if n < len(sent) - 1:
            g_now, taps_now, *blocks = call(
                functools.partial(weight_kernel, col, scale),
                [like((rows, width), BF16), like((rows, 3 * width), BF16)]
                + [like((chans // 2, 3 * width), BF16)] * 2,
                (shift, top, h_t) + recv,
                    flops=unit * width // chans,
            )
            acc = call(
                functools.partial(back_kernel, col),
                [like((rows, chans), F32)],
                (taps_now, weight),
                flops=10**11,
            )[0]
            used.append(g_now)
            accs.append(acc)
        else:
            *blocks, grad = call(
                functools.partial(last_kernel, col, scale, len(used)),
                [like((chans // 2, 3 * width + 128), BF16)] * 2 + [like(x.shape, BF16)],
                (shift, top, h_t, weight, hot) + recv + tuple(used) + tuple(accs),
                    scratch=[pltpu.VMEM((rows, 3 * width), BF16)],
                flops=10**11,
            )
        reduce_by, gather_by = CHAINS[n]
        levels = reduce_by(inner)
        rounds = []

        def ordered(*arrived):
            arrived = list(arrived)
            at = TIES.get(len(rounds))
            rounds.append(arrived)
            if before and at is not None:
                arrived = list(lax.optimization_barrier((*arrived, *before[at]))[: len(arrived)])
            return arrived

        if before and FIRST:
            blocks[1] = lax.optimization_barrier((blocks[1], *before[1]))[0]
        blocks = [blocks[0]] + ordered(swap(blocks[1], 1))
        for level in levels:
            split = 1 << len(level[0])
            blocks = call(
                functools.partial(fold_kernel, level, len(blocks)),
                [like((blocks[0].shape[0] // split, blocks[0].shape[1]), BF16)] * split,
                tuple(blocks),
            )
            ahead = blocks[1]
            arrived = [
                swap(blocks[o], *(mask_of(bits, o) for bits in level)) for o in offsets_in(level)
            ]
            blocks = [blocks[0]] + ordered(*arrived)
        keep = sum(v.astype(F32) for v in blocks).astype(BF16)
        arrived = ordered(swap(keep, 1 << (dp_bits - 1)))
        own = (keep.astype(F32) + arrived[0].astype(F32)).astype(BF16)
        held = [(own, [(0, (0, 0))])]
        for level in reversed(gather_by(inner)):
            message = jnp.concatenate([v for v, _ in held], axis=0) if len(held) > 1 else own
            offsets = [m for _, offs in held for _, m in offs]
            masks = [tuple(mask_of(bits, o) for bits in level) for o in offsets_in(level)]
            arrived = ordered(*(swap(message, *mask) for mask in masks))
            held += [
                (v, [(0, (m[0] ^ e, m[1] ^ o)) for m in offsets]) for v, (e, o) in zip(arrived, masks)
            ]
        gathered.append((width, levels, held))
        before = rounds

    both = [jnp.concatenate([v for v, _ in held], axis=0) for _, _, held in gathered]
    crossed = swap(jnp.concatenate(both, axis=1), 1)
    plans = []
    pieces = []
    at = 0
    for width, levels, held in gathered:
        lists = [(0, offs) for _, offs in held] + [(at, [(1, m) for _, offs in held for _, m in offs])]
        plans.append((width, held[0][0].shape[1], levels, lists))
        pieces += [v for v, _ in held] + [crossed]
        at += held[0][0].shape[1]

    weight_out, table_out = call(
        functools.partial(assemble_kernel, plans),
        [like(weight.shape, BF16), like(table.shape, BF16)],
        tuple(pieces),
        scratch=[pltpu.VMEM((chans, 128), F32)],
    )
    return (grad[None], weight_out[None], table_out[None])


CHAINS = ((single, single), (single, double))
TIES = {4: 5}
FIRST = True
HOLD = False


def solution(mesh):
    placed = (
        P("section", "dp", None, None),
        P("dp", None, None),
        P("section", None, None, None),
        P("section", None, None),
        P("dp"),
        P("section"),
    )
    return jax.shard_map(
        body,
        mesh=mesh,
        in_specs=placed,
        out_specs=(
            P("section", "dp", None, None),
            P("section", None, None, None),
            P("section", None, None),
        ),
        check_vma=False,
    )
```

```python
import functools
import math

import jax
import jax.numpy as jnp
from jax import lax
from jax.experimental import pallas as pl
from jax.experimental.pallas import tpu as pltpu
from jax.sharding import PartitionSpec as P

SENT = (256, 256)
PARTS = 2
F32 = jnp.float32
BF16 = jnp.bfloat16
VMEM = pl.BlockSpec(memory_space=pltpu.VMEM)
SMEM = pl.BlockSpec(memory_space=pltpu.SMEM)
HBM = pl.BlockSpec(memory_space=pltpu.HBM)
NT = (((1,), (1,)), ((), ()))


def call(kernel, out_shape, args, smem=0, far=0, scratch=(), flops=0):
    specs = [SMEM] * smem + [HBM] * far + [VMEM] * (len(args) - smem - far)
    moved = sum(a.size * a.dtype.itemsize for a in args)
    moved += sum(math.prod(o.shape) * o.dtype.itemsize for o in out_shape)
    return pl.pallas_call(
        kernel,
        out_shape=out_shape,
        in_specs=specs,
        out_specs=[VMEM] * len(out_shape),
        scratch_shapes=list(scratch),
        compiler_params=pltpu.CompilerParams(vmem_limit_bytes=32 * 2**20),
        cost_estimate=pl.CostEstimate(flops=flops, bytes_accessed=moved, transcendentals=0),
    )(*args)


def is_top():
    return lax.axis_index("section") == lax.axis_size("section") - 1


def dp_bit(n):
    return lax.rem(lax.div(lax.axis_index("dp"), 1 << n), 2)


def like(shape, dtype):
    return jax.ShapeDtypeStruct(shape, dtype)


def shift_matrix(bins, dilation):
    row = lax.broadcasted_iota(jnp.int32, (bins, bins), 0)
    col = lax.broadcasted_iota(jnp.int32, (bins, bins), 1)
    both = [jnp.where(col == row + by, 1.0, 0.0).astype(BF16) for by in (-dilation, dilation)]
    return jnp.concatenate(both, axis=0)


def put_taps(values, taps, shift, orientation):
    rows, cols = values.shape
    bins = shift.shape[1]
    taps[:, cols : 2 * cols] = values
    for b in range(rows // bins):
        at = slice(b * bins, (b + 1) * bins)
        moved = jnp.dot(shift[...], values[at], preferred_element_type=F32).astype(BF16)
        earlier, later = moved[:bins], moved[bins:]
        first, third = (earlier, later) if orientation == 1 else (later, earlier)
        taps[at, 0:cols] = first
        taps[at, 2 * cols : 3 * cols] = third


def back_product(taps, weight, cols):
    total = None
    for k in range(3):
        part = lax.dot_general(
            taps[:, k * cols : (k + 1) * cols], weight[k], NT, preferred_element_type=F32
        )
        total = part if total is None else total + part
    return total


def forward(h, taps, shift, weight, slope, wait=None):
    put_taps(h, taps, shift, 1)
    chans = h.shape[1]
    y = None
    for k in range(3):
        if wait is not None:
            wait(k)
        part = jnp.dot(taps[:, k * chans : (k + 1) * chans], weight[k], preferred_element_type=F32)
        y = part if y is None else y + part
    gate = jax.nn.sigmoid(y)
    slope[...] = gate * (1.0 + y * (1.0 - gate))


def backward(g, taps, shift, slope):
    delta = (g * slope[...]).astype(BF16)
    put_taps(delta, taps, shift, -1)


def below_of(g, taps, weight, col, out):
    cols = slice(col, col + out.shape[1])
    dh = back_product(taps, weight[:, cols, :], weight.shape[2])
    out[...] = (g[:, cols].astype(F32) + dh).astype(BF16)


def first_kernel(dil, ts, x, table, weight, top, mixed, weight_v, top_v, hot, shift, *rest):
    slope, taps, g_out, ts_s, x_v, table_v, tab, forward_taps, sems = rest
    groups, bins, chans = x.shape
    rows = slope.shape[0]
    near = slice(0, rows // bins)
    others = slice(rows // bins, groups)
    pairs = [(ts, ts_s), (table, table_v), (x.at[near], x_v.at[near])]
    pairs += [(weight.at[k], weight_v.at[k]) for k in range(3)]
    pairs += [(top.at[near], top_v.at[near]), (x.at[others], x_v.at[others]), (top.at[others], top_v.at[others])]
    copies = [pltpu.make_async_copy(a, b, sems.at[n]) for n, (a, b) in enumerate(pairs)]
    for copy in copies:
        copy.start()
    shift[...] = shift_matrix(bins, dil[0])
    for copy in copies[:3]:
        copy.wait()
    tab[...] = table_v[...].astype(F32)

    def mix(b):
        row = x_v[b].astype(F32) + tab[pl.ds(ts_s[b], 1), :]
        mixed[b * bins : (b + 1) * bins, :] = row.astype(BF16)

    for b in range(rows // bins):
        mix(b)

    @pl.when(is_top())
    def _():
        def arrived(k):
            copies[3 + k].wait()

        forward(mixed[0:rows, :], forward_taps, shift, weight_v, slope, arrived)
        copies[6].wait()
        g = top_v[near].reshape(rows, chans)
        backward(g.astype(F32), taps, shift, slope)
        below_of(g, taps, weight_v, 0, g_out)

    @pl.when(jnp.logical_not(is_top()))
    def _():
        for copy in copies[3:7]:
            copy.wait()
        g_out[...] = jnp.zeros(g_out.shape, BF16)

    steps = lax.broadcasted_iota(jnp.int32, hot.shape, 0)
    lanes = lax.broadcasted_iota(jnp.int32, hot.shape, 1)
    marks = jnp.zeros(hot.shape, F32)
    for b in range(groups):
        marks = jnp.where((lanes == b) & (steps == ts_s[b]), 1.0, marks)
    hot[...] = marks
    copies[7].wait()
    for b in range(rows // bins, groups):
        mix(b)
    copies[8].wait()


def other_kernel(start, shift, mixed, weight, top, slope, taps, g_out, forward_taps):
    @pl.when(is_top())
    def _():
        at = slice(start, start + slope.shape[0])
        forward(mixed[at, :], forward_taps, shift, weight, slope)
        g = top[...].reshape(mixed.shape)[at]
        backward(g.astype(F32), taps, shift, slope)
        below_of(g, taps, weight, 0, g_out)

    @pl.when(jnp.logical_not(is_top()))
    def _():
        g_out[...] = jnp.zeros(g_out.shape, BF16)


def rest_kernel(col, weight, top, *rest):
    taps, g_out = rest[:-1], rest[-1]
    part = taps[0].shape[0]

    @pl.when(is_top())
    def _():
        g = top[...].reshape(-1, top.shape[2])
        for n, ref in enumerate(taps):
            at = slice(n * part, (n + 1) * part)
            below_of(g[at], ref, weight, col, g_out.at[at])

    @pl.when(jnp.logical_not(is_top()))
    def _():
        g_out[...] = jnp.zeros(g_out.shape, BF16)


def prepare_kernel(shift, mixed, weight, *rest):
    early, h_t, late, taps = rest[:PARTS], rest[PARTS], rest[PARTS + 1 : -1], rest[-1]
    part = taps.shape[0]
    h_t[...] = mixed[...].T

    @pl.when(is_top())
    def _():
        for n in range(PARTS):
            late[n][...] = early[n][...]

    @pl.when(jnp.logical_not(is_top()))
    def _():
        for n in range(PARTS):
            forward(mixed[n * part : (n + 1) * part, :], taps, shift, weight, late[n])


def layer_kernel(start, shift, slope, weight, top, *rest):
    early, late, out, out_late, taps = rest
    rows = slope.shape[0]
    got = jnp.concatenate([early[...], late[start : start + rows]], axis=1)
    fresh = top[...].reshape(-1, top.shape[2])[start : start + rows]
    g = jnp.where(is_top(), fresh.astype(F32), got.astype(F32))
    backward(g, taps, shift, slope)
    below_of(g, taps, weight, 0, out)
    below_of(g, taps, weight, out.shape[1], out_late)


def upstream(col, top, recv):
    got = [ref[...].astype(F32) for ref in recv]
    got = got[0] if len(got) == 1 else jnp.concatenate(got, axis=0)
    rows, width = got.shape
    fresh = top[...].reshape(rows, top.shape[-1])[:, col : col + width]
    return jnp.where(is_top(), fresh.astype(F32), got)


def delta_of(g, slope, col):
    width = g.shape[1]
    factor = jnp.concatenate([ref[:, col : col + width] for ref in slope], axis=0)
    return (g * factor).astype(BF16)


def by_core(even, odd, other=False):
    return jnp.where(dp_bit(0) == (1 if other else 0), even, odd)


def place_in(bits, mask=0):
    place = 0
    for n in reversed(bits):
        place = place * 2 + (1 - dp_bit(n) if (mask >> n) & 1 else dp_bit(n))
    return place


def mask_of(bits, offset):
    return sum(1 << n for j, n in enumerate(bits) if (offset >> j) & 1)


def weight_blocks(h_t, taps, scale, keep, send, cols):
    half = h_t.shape[0] // 2
    bit = dp_bit(0)
    for ref, part in ((keep, bit), (send, 1 - bit)):
        left = h_t[pl.ds(pl.multiple_of(part * half, half), half), :]
        prod = jnp.dot(left, taps[...], preferred_element_type=F32)
        ref[:, 0:cols] = (prod * scale).astype(BF16)


def weight_half(h_t, taps, scale, part, out):
    half = out.shape[0]
    left = h_t[pl.ds(pl.multiple_of(part * half, half), half), :]
    out[...] = (jnp.dot(left, taps[...], preferred_element_type=F32) * scale).astype(BF16)


def keep_kernel(scale, h_t, taps, keep):
    weight_half(h_t, taps, scale, dp_bit(0), keep)


def weight_kernel(col, scale, shift, top, h_t, *rest):
    slope, recv, out = rest[:PARTS], rest[PARTS:-3], rest[-3:]
    g_used, taps, send = out
    width = g_used.shape[1]
    g = upstream(col, top, recv)
    g_used[...] = g.astype(BF16)
    delta = delta_of(g, slope, col)
    put_taps(delta, taps, shift, -1)
    weight_half(h_t, taps, scale, 1 - dp_bit(0), send)


def back_kernel(col, taps, weight, acc):
    width = taps.shape[1] // 3
    acc[...] = back_product(taps, weight[:, :, col : col + width], width)


def last_kernel(col, scale, prior, shift, top, h_t, weight, hot, *rest):
    slope, recv = rest[:PARTS], rest[PARTS : -4 - 2 * prior]
    g_prior, acc = rest[-4 - 2 * prior : -4 - prior], rest[-4 - prior : -4]
    keep, send, grad, taps = rest[-4:]
    groups, bins, chans = grad.shape
    width = taps.shape[1] // 3
    g = upstream(col, top, recv)
    delta = delta_of(g, slope, col)
    put_taps(delta, taps, shift, -1)
    dh = back_product(taps, weight[:, :, col : col + width], width)
    for ref in acc:
        dh = dh + ref[...]
    whole = jnp.concatenate([ref[...].astype(F32) for ref in g_prior] + [g], axis=1)
    grad[...] = (whole + dh).astype(BF16).reshape(groups, bins, chans)
    table = jnp.zeros((hot.shape[0], chans), F32)
    for b in range(groups):
        total = jnp.sum(dh[b * bins : (b + 1) * bins], axis=0, keepdims=True)
        table = table + hot[:, b : b + 1] * (total * scale)
    table_t = table.T.astype(BF16)
    weight_blocks(h_t, taps, scale, keep, send, 3 * width)
    half = chans // 2
    bit = dp_bit(0)
    for ref, part in ((send, 1 - bit), (keep, bit)):
        ref[:, 3 * width :] = jnp.where(part == 0, table_t[0:half], table_t[half:])


def fold_kernel(level, count, *refs):
    summands, out = refs[:count], refs[count:]
    size = out[0].shape[0]
    for offset, ref in enumerate(out):
        part = by_core(*(place_in(bits, mask_of(bits, offset)) for bits in level))
        at = pl.ds(pl.multiple_of(part * size, size), size)
        total = summands[0][at, :].astype(F32)
        for other in summands[1:]:
            total = total + other[at, :].astype(F32)
        ref[...] = total.astype(BF16)


def assemble_kernel(plans, *refs):
    weight_out, table_out, table_t = refs[-3:]
    pieces = list(refs[:-3])
    col = 0
    for width, total, levels, lists in plans:
        for left, offsets in lists:
            ref = pieces.pop(0)
            size = ref.shape[0] // len(offsets)
            for slot, (core, masks) in enumerate(offsets):
                blocks = []
                for parity in (0, 1):
                    block = 0
                    for level in levels:
                        bits = level[parity]
                        block = block * (1 << len(bits)) + place_in(bits, masks[parity])
                    blocks.append(block)
                block = by_core(*blocks, other=core == 1)
                half = dp_bit(0) if core == 0 else 1 - dp_bit(0)
                block = block + half * (weight_out.shape[1] // 2 // size)
                row = pl.ds(pl.multiple_of(block * size, size), size)
                here = slice(slot * size, (slot + 1) * size)
                for k in range(3):
                    weight_out[k, row, col : col + width] = ref[
                        here, left + k * width : left + (k + 1) * width
                    ]
                if total > 3 * width:
                    table_t[row, :] = ref[here, left + 3 * width : left + total].astype(F32)
        col += width
    table_out[...] = table_t[...].T[: table_out.shape[0]].astype(BF16)


def swap(value, even, odd=None):
    count = lax.axis_size("dp")
    masks = (even, even if odd is None else odd)
    return lax.ppermute(value, "dp", [(i, i ^ masks[i % 2]) for i in range(count)])


def single(bits):
    return [((a,), (b,)) for a, b in zip(bits, reversed(bits))]


def double(bits):
    pairs = [tuple(bits[n : n + 2]) for n in range(0, len(bits), 2)]
    return [(pair, pair) for pair in pairs]


def offsets_in(level):
    return range(1, 1 << len(level[0]))


def body(section_input, top_grad, conv_weight, step_table, timesteps, dilations):
    section_count = lax.axis_size("section")
    dp_count = lax.axis_size("dp")
    dp_bits = dp_count.bit_length() - 1
    x = section_input[0]
    weight = conv_weight[0]
    table = step_table[0]
    groups, bins, chans = x.shape
    rows = groups * bins
    sent = SENT
    scale = 1.0 / math.sqrt(groups * dp_count * bins)
    unit = 2 * rows * chans * chans * 3
    starts = [sum(sent[:n]) for n in range(len(sent))]

    part = rows // PARTS
    room = pltpu.VMEM((part, 3 * chans), BF16)
    of_part = [
        like((part, chans), F32),
        like((part, 3 * chans), BF16),
        like((part, sent[0]), BF16),
    ]
    far = (timesteps, x, table, weight, top_grad)
    mixed, weight, top, hot, shift, *first = call(
        first_kernel,
        [
            like((rows, chans), BF16),
            like(weight.shape, BF16),
            like(x.shape, BF16),
            like((128, 128), F32),
            like((2 * bins, bins), BF16),
        ]
        + of_part,
        (dilations,) + tuple(pltpu.with_memory_space_constraint(v, pltpu.HBM) for v in far),
        smem=1,
        far=5,
        scratch=[
            pltpu.SMEM(timesteps.shape, jnp.int32),
            pltpu.VMEM(x.shape, BF16),
            pltpu.VMEM(table.shape, BF16),
            pltpu.VMEM(table.shape, F32),
            room,
            pltpu.SemaphoreType.DMA((9,)),
        ],
        flops=2 * unit // PARTS,
    )

    def below(value):
        pairs = [(i, i - 1) for i in range(1, section_count)]
        if section_count == 2:
            pairs.append((0, 1))
        return lax.ppermute(value, "section", pairs)

    made = [first]
    for n in range(1, PARTS):
        made.append(
            call(
                functools.partial(other_kernel, n * part),
                of_part,
                (shift, mixed, weight, top),
                scratch=[room],
                flops=2 * unit // PARTS,
            )
        )
    slope = [v[0] for v in made]
    late = call(
        functools.partial(rest_kernel, sent[0]),
        [like((rows, sent[1]), BF16)],
        (weight, top) + tuple(v[1] for v in made),
        flops=unit // 2,
    )[0]
    got = [[below(v[2]) for v in made], [below(late)]]
    h_t, *slope = call(
        prepare_kernel,
        [like((chans, rows), BF16)] + [like((part, chans), F32)] * PARTS,
        (shift, mixed, weight) + tuple(slope),
        scratch=[room],
        flops=unit // 9,
    )
    for _ in range(section_count - 2):
        pieces = [
            call(
                functools.partial(layer_kernel, n * part),
                [like((part, cols), BF16) for cols in sent],
                (shift, slope[n], weight, top, got[0][n], got[1][0]),
                scratch=[room],
                flops=unit // PARTS,
            )
            for n in range(PARTS)
        ]
        late = jnp.concatenate([v[1] for v in pieces], axis=0)
        got = [[below(v[0]) for v in pieces], [below(late)]]

    inner = list(range(1, dp_bits - 1))
    gathered = []
    before = []
    ahead = None
    used = []
    accs = []
    for n, width in enumerate(sent):
        col = starts[n]
        if ahead is not None and HOLD:
            got[n], _ = lax.optimization_barrier((got[n], ahead))
        recv = tuple(slope) + tuple(got[n])
        if n < len(sent) - 1:
            g_now, taps_now, send = call(
                functools.partial(weight_kernel, col, scale),
                [like((rows, width), BF16), like((rows, 3 * width), BF16)]
                + [like((chans // 2, 3 * width), BF16)],
                (shift, top, h_t) + recv,
                    flops=unit * width // chans,
            )
            keep = call(
                functools.partial(keep_kernel, scale),
                [like((chans // 2, 3 * width), BF16)],
                (h_t, taps_now),
                flops=unit * width // chans // 2,
            )[0]
            blocks = [keep, send]
            acc = call(
                functools.partial(back_kernel, col),
                [like((rows, chans), F32)],
                (taps_now, weight),
                flops=10**11,
            )[0]
            used.append(g_now)
            accs.append(acc)
        else:
            *blocks, grad = call(
                functools.partial(last_kernel, col, scale, len(used)),
                [like((chans // 2, 3 * width + 128), BF16)] * 2 + [like(x.shape, BF16)],
                (shift, top, h_t, weight, hot) + recv + tuple(used) + tuple(accs),
                    scratch=[pltpu.VMEM((rows, 3 * width), BF16)],
                flops=10**11,
            )
        reduce_by, gather_by = CHAINS[n]
        levels = reduce_by(inner)
        rounds = []

        def ordered(*arrived):
            arrived = list(arrived)
            at = TIES.get(len(rounds))
            rounds.append(arrived)
            if before and at is not None:
                arrived = list(lax.optimization_barrier((*arrived, *before[at]))[: len(arrived)])
            return arrived

        if before and FIRST:
            blocks[1] = lax.optimization_barrier((blocks[1], *before[1]))[0]
        blocks = [blocks[0]] + ordered(swap(blocks[1], 1))
        for level in levels:
            split = 1 << len(level[0])
            blocks = call(
                functools.partial(fold_kernel, level, len(blocks)),
                [like((blocks[0].shape[0] // split, blocks[0].shape[1]), BF16)] * split,
                tuple(blocks),
            )
            ahead = blocks[1]
            arrived = [
                swap(blocks[o], *(mask_of(bits, o) for bits in level)) for o in offsets_in(level)
            ]
            blocks = [blocks[0]] + ordered(*arrived)
        keep = sum(v.astype(F32) for v in blocks).astype(BF16)
        arrived = ordered(swap(keep, 1 << (dp_bits - 1)))
        own = (keep.astype(F32) + arrived[0].astype(F32)).astype(BF16)
        held = [(own, [(0, (0, 0))])]
        for level in reversed(gather_by(inner)):
            message = jnp.concatenate([v for v, _ in held], axis=0) if len(held) > 1 else own
            offsets = [m for _, offs in held for _, m in offs]
            masks = [tuple(mask_of(bits, o) for bits in level) for o in offsets_in(level)]
            arrived = ordered(*(swap(message, *mask) for mask in masks))
            held += [
                (v, [(0, (m[0] ^ e, m[1] ^ o)) for m in offsets]) for v, (e, o) in zip(arrived, masks)
            ]
        gathered.append((width, levels, held))
        before = rounds

    both = [jnp.concatenate([v for v, _ in held], axis=0) for _, _, held in gathered]
    crossed = swap(jnp.concatenate(both, axis=1), 1)
    plans = []
    pieces = []
    at = 0
    for width, levels, held in gathered:
        lists = [(0, offs) for _, offs in held] + [(at, [(1, m) for _, offs in held for _, m in offs])]
        plans.append((width, held[0][0].shape[1], levels, lists))
        pieces += [v for v, _ in held] + [crossed]
        at += held[0][0].shape[1]

    weight_out, table_out = call(
        functools.partial(assemble_kernel, plans),
        [like(weight.shape, BF16), like(table.shape, BF16)],
        tuple(pieces),
        scratch=[pltpu.VMEM((chans, 128), F32)],
    )
    return (grad[None], weight_out[None], table_out[None])


CHAINS = ((single, single), (single, double))
TIES = {4: 5}
FIRST = True
HOLD = False


def solution(mesh):
    placed = (
        P("section", "dp", None, None),
        P("dp", None, None),
        P("section", None, None, None),
        P("section", None, None),
        P("dp"),
        P("section"),
    )
    return jax.shard_map(
        body,
        mesh=mesh,
        in_specs=placed,
        out_specs=(
            P("section", "dp", None, None),
            P("section", None, None, None),
            P("section", None, None),
        ),
        check_vma=False,
    )
```
